256 devices in a mesh: dap: 128 (over y_lo, z, x, core), dp: 2 (over y_hi).
Axes of the slice: x: 4, y: 4 (y_hi: 2, y_lo: 2; y = y_hi * 2 + y_lo), z: 8, core: 2. Of those that a mesh axis runs over, the one named last changes fastest.
Arguments:
- pair: bfloat16 [1024, 512, 128], P(('dp', 'dap')), parts along dimension 0, may hold values from -6 to 6
- valid: int32 [2], P('dp'), parts along dimension 0, may hold values from 256 to 512
- w_query: bfloat16 [2, 128, 128], replicated, as said below
- w_key: bfloat16 [2, 128, 128], replicated, as said below
- w_value: bfloat16 [2, 128, 128], replicated, may hold values from -0.5 to 0.5
- w_gate: bfloat16 [2, 128, 128], replicated, may hold values from -0.5 to 0.5
- w_bias: bfloat16 [2, 128, 4], replicated, may hold values from -0.5 to 0.5
- w_out: bfloat16 [2, 128, 128], replicated, may hold values from -0.5 to 0.5
Outputs:
- mixed: bfloat16 [1024, 512, 128], P(('dp', 'dap')), parts along dimension 0
The draws below stay inside these ranges and needn't reach their ends.
There are 2 independent parts, one for each index of `dp`. The reference program is written for one: setup_inputs(seed, part) draws one part's arguments, and reference() takes and returns one part's arrays. A program takes and returns all parts, laid end to end along the dimension named above; an argument that names none is the same for every part. Nothing has to cross between parts.
Inputs may be any that keep to these rules, and one draw needn't show every extreme that they name: pair rows and columns of index 511 down to valid are padding; they are masked as keys. `w_query`: a weight matrix of 128 rows; in some draws its entries are up to some tens of times the fan-in scale and correlated with w_key, so that scores may reach a few hundred. `w_key`: a weight matrix of 128 rows scaled by its fan-in.
All inputs are finite; a program needn't handle non-finite values.
Results may differ from the reference program's by a relative error of at most 0.015.
Values may be sent and summed in bfloat16 or wider, within the bound.
No kernel may reach another device: no remote copies, remote signals or barrier semaphores. Data moves between devices by JAX's collectives and lax.ppermute only.
A program may use at most 64 MiB of HBM per device.

```python
import math
import jax
import jax.numpy as jnp
from jax import lax

C = 128
HEADS = 4
HEAD_DIM = 32
HD = 128
TOKENS = 512


def shared_keys(key):
    return jax.random.normal(jax.random.fold_in(key, 101), (2, C, HD), jnp.float32) / math.sqrt(C)


def draw_w_key(key, part):
    base = shared_keys(key)
    return base.astype(jnp.bfloat16)


def draw_w_query(key, part):
    key = jax.random.fold_in(key, 2)
    fresh = jax.random.normal(key, (2, C, HD), jnp.float32) / math.sqrt(C)
    result = fresh
    return result.astype(jnp.bfloat16)


def levels(own_key, shape, pieces, least, high):
    def one(dim, blocks):
        draws = jax.random.uniform(jax.random.fold_in(jax.random.fold_in(own_key, 6), dim), (blocks,), jnp.float32, least / len(pieces), high / len(pieces))
        return jnp.repeat(jnp.exp(draws), shape[dim] // blocks).reshape((-1,) + (1,) * (len(shape) - dim - 1))

    gain = one(*pieces[0])
    for cut in pieces[1:]:
        gain = gain * one(*cut)
    return gain


def gaussian(own_key, extent, deviation, limit, split=(), kind=jnp.bfloat16):
    array = deviation * jax.random.normal(own_key, extent, jnp.float32)
    if split:
        array = array * levels(own_key, extent, split, -0.22, 0.18)
    return jnp.clip(array, -limit, limit).astype(kind)


def setup_inputs(seed: int = 0, part: int = 0) -> dict:
    key_of = jax.random.split(jax.random.key(seed), 9)
    part_keys = jax.random.split(jax.random.fold_in(key_of[8], part), 9)
    pair = gaussian(part_keys[0], (TOKENS, TOKENS, C), 1.0, 6.0, ((0, 128),))
    valid = jax.random.randint(part_keys[1], (1,), TOKENS // 2, TOKENS + 1).astype(jnp.int32)
    w_query = draw_w_query(jax.random.fold_in(key_of[8], 71), part)
    w_key = draw_w_key(jax.random.fold_in(key_of[8], 71), part)
    w_value = gaussian(key_of[4], (2, C, HD), C ** -0.5, 0.5)
    w_gate = gaussian(key_of[5], (2, C, HD), C ** -0.5, 0.5)
    w_bias = gaussian(key_of[6], (2, C, HEADS), C ** -0.5, 0.5)
    w_out = gaussian(key_of[7], (2, HD, C), HD ** -0.5, 0.5)
    return dict(pair=pair, valid=valid, w_query=w_query, w_key=w_key, w_value=w_value, w_gate=w_gate, w_bias=w_bias, w_out=w_out)


epsilon = 1e-05
masked_value = -1000000000.0

def layer_normed(values):
    wide = values.astype(jnp.float32)
    center = lax.optimization_barrier(jnp.mean(wide, axis=-1, keepdims=True))
    spread = lax.optimization_barrier(jnp.mean(jnp.square(wide - center), axis=-1, keepdims=True))
    return ((wide - center) * lax.rsqrt(spread + epsilon)).astype(jnp.bfloat16)

def attend(queries, key_rows, value_rows, gate_logits, bias_term, key_mask, w_output):
    count = queries.shape[0]
    heads = bias_term.shape[0]
    query_heads = queries.reshape(count, heads, -1).astype(jnp.float32)
    key_heads = key_rows.reshape(key_rows.shape[0], heads, -1).astype(jnp.float32)
    value_heads = value_rows.reshape(value_rows.shape[0], heads, -1).astype(jnp.float32)
    scores = jnp.einsum('qhd,khd->hqk', query_heads, key_heads)
    scores = scores + bias_term.astype(jnp.float32) + key_mask[None, None, :]
    highest = lax.optimization_barrier(jnp.max(scores, axis=-1, keepdims=True))
    expsum = jnp.exp(scores - highest)
    probs = (expsum / lax.optimization_barrier(jnp.sum(expsum, axis=-1, keepdims=True))).astype(jnp.bfloat16)
    mixed_heads = jnp.einsum('hqk,khd->qhd', probs.astype(jnp.float32), value_heads)
    gated = (jax.nn.sigmoid(gate_logits) * mixed_heads.reshape(count, -1)).astype(jnp.bfloat16)
    return jnp.dot(gated, w_output, preferred_element_type=jnp.float32)

def branch(layout, valid, w_query, w_key, w_value, w_gate, w_bias, w_output):
    normed = layer_normed(layout)
    bias_all = jnp.einsum('ijc,ch->hij', normed.astype(jnp.float32), w_bias.astype(jnp.float32)).astype(jnp.bfloat16)
    positions = jnp.arange(layout.shape[1]).astype(jnp.int32)
    key_mask = jnp.where(positions < valid[0], 0.0, masked_value).astype(jnp.float32)
    scale = 1.0 / math.sqrt(HEAD_DIM)

    def one_row(row):
        queries = (jnp.dot(row, w_query, preferred_element_type=jnp.float32) * scale).astype(jnp.bfloat16)
        key_rows = jnp.dot(row, w_key, preferred_element_type=jnp.float32).astype(jnp.bfloat16)
        value_rows = jnp.dot(row, w_value, preferred_element_type=jnp.float32).astype(jnp.bfloat16)
        gate_logits = jnp.dot(row, w_gate, preferred_element_type=jnp.float32)
        return attend(queries, key_rows, value_rows, gate_logits, bias_all, key_mask, w_output)
    return lax.map(one_row, normed)

def reference(pair, valid, w_query, w_key, w_value, w_gate, w_bias, w_out):
    first = branch(pair, valid, w_query[0], w_key[0], w_value[0], w_gate[0], w_bias[0], w_out[0])
    section_one = (pair.astype(jnp.float32) + first).astype(jnp.bfloat16)
    second = branch(jnp.swapaxes(section_one, 0, 1), valid, w_query[1], w_key[1], w_value[1], w_gate[1], w_bias[1], w_out[1])
    second = lax.optimization_barrier(second.astype(jnp.bfloat16))
    return (section_one.astype(jnp.float32) + jnp.swapaxes(second, 0, 1).astype(jnp.float32)).astype(jnp.bfloat16)
```

```python
import functools
import math

import jax
import jax.numpy as jnp
from jax import lax
from jax.experimental import pallas as pl
from jax.experimental.pallas import tpu as pltpu
from jax.sharding import Mesh, PartitionSpec as P

HEAD_DIM = 32
EPSILON = 1e-05
MASKED = -1000000000.0
CHIPS = ("y", "z", "x")
VMEM_LIMIT = 48 * 1024 * 1024

SMEM = pl.BlockSpec(memory_space=pltpu.SMEM)


def params():
    return pltpu.CompilerParams(vmem_limit_bytes=VMEM_LIMIT)


def layer_normed(wide):
    center = jnp.mean(wide, axis=-1, keepdims=True)
    moved = wide - center
    spread = jnp.mean(jnp.square(moved), axis=-1, keepdims=True)
    return moved * lax.rsqrt(spread + EPSILON)


def head_bias(normed, wb, place, tokens):
    both = lax.dot_general(
        wb, normed, (((1,), (1,)), ((), ())), preferred_element_type=jnp.float32
    )
    first = place[0] == 0
    return (
        jnp.where(first, both[0:1], both[2:3]),
        jnp.where(first, both[1:2], both[3:4]),
    )


def masked_bias(rows, place):
    positions = lax.broadcasted_iota(jnp.int32, rows.shape, 1)
    return jnp.where(positions < place[2], rows, MASKED).astype(jnp.bfloat16)


def prepare_rows(place, sib_ref, own_ref, wb_ref, normed_ref, bias_ref, rows_ref):
    core = place[0]
    count, tokens, _ = own_ref.shape
    for half, (ref, at) in enumerate(((sib_ref, 1 - core), (own_ref, core))):
        for r in range(count):
            normed = layer_normed(ref[r].astype(jnp.float32)).astype(jnp.bfloat16)
            normed_ref[half * count + r] = normed
            one, two = head_bias(normed, wb_ref[...], place, tokens)
            rows_ref[pl.ds(at * count + r, 1), :] = one
            rows_ref[pl.ds((2 + at) * count + r, 1), :] = two
    bias_ref[...] = masked_bias(rows_ref[...], place)


def prepare_columns(place, own_ref, sib_ref, wb_ref, normed_ref, bias_ref, rows_ref, wide_ref):
    core = place[0]
    chips, count, width, channels = own_ref.shape
    tokens = chips * 2 * count
    for ref, at in ((own_ref, core), (sib_ref, 1 - core)):
        wide_ref[:, pl.ds(at, 1)] = ref[...].astype(jnp.float32)[:, None]
    flat = wide_ref.reshape(tokens, width, channels)
    for j in range(width):
        normed = flat[:, j, :].astype(jnp.bfloat16)
        normed_ref[j] = normed
        one, two = head_bias(normed, wb_ref[...], place, tokens)
        rows_ref[pl.ds(j, 1), :] = one
        rows_ref[pl.ds(width + j, 1), :] = two
    bias_ref[...] = masked_bias(rows_ref[...], place)


def load_bias(place, pieces, wide_ref):
    for step, ref in enumerate(pieces):
        spot = place[3 + step]
        rows = ref.shape[1] // 2
        wide = ref[...].astype(jnp.float32)
        wide_ref[0, :, pl.ds(spot, 1)] = wide[:, None, :rows]
        wide_ref[1, :, pl.ds(spot, 1)] = wide[:, None, rows:]


def attend(place, normed, w_ref, bias_ref, chunk):
    core = place[0]
    tokens, channels = normed.shape
    projected = jnp.dot(normed, w_ref[...], preferred_element_type=jnp.float32)
    scale = 1.0 / math.sqrt(HEAD_DIM)
    query = (projected[:, :channels] * scale).astype(jnp.bfloat16)
    key_t = projected[:, channels : 2 * channels].T.astype(jnp.bfloat16)
    value = projected[:, 2 * channels : 3 * channels].astype(jnp.bfloat16)
    gate = projected[:, 3 * channels :]
    lane_head = lax.broadcasted_iota(jnp.int32, (tokens, channels), 1) // HEAD_DIM
    queries, values = [], []
    for h in range(2):
        head = 2 * core + h
        mine = lane_head == head
        queries.append(jnp.where(mine, query, jnp.zeros_like(query)))
        ones = jnp.where(lane_head == (head + 2) % 4, 1.0, 0.0).astype(jnp.bfloat16)
        values.append(jnp.where(mine, value, ones))
    parts = []
    for at in range(0, tokens, chunk):
        total = None
        for h in range(2):
            score = jnp.dot(
                queries[h][at : at + chunk], key_t, preferred_element_type=jnp.float32
            )
            score = score + bias_ref[h, at : at + chunk, :]
            highest = jnp.max(score, axis=-1, keepdims=True)
            weight = jnp.exp(score - highest).astype(jnp.bfloat16)
            out = jnp.dot(weight, values[h], preferred_element_type=jnp.float32)
            total = out if total is None else total + out
        sums = pltpu.roll(total, channels // 2, 1)
        part = jax.nn.sigmoid(gate[at : at + chunk]) * total / sums
        parts.append(jnp.where(lane_head[at : at + chunk] // 2 == core, part, 0.0))
    return jnp.concatenate(parts, axis=0)


def attend_rows(place, normed_ref, w_ref, b0, b1, b2, b3, sib_ref, own_ref, wide_ref):
    step = pl.program_id(0)

    @pl.when(step == 0)
    def _():
        load_bias(place, (b0, b1, b2, b3), wide_ref)

    tokens = normed_ref.shape[1]
    bias = wide_ref.reshape(2, tokens, tokens)
    gated = attend(place, normed_ref[0], w_ref, bias, 128).astype(jnp.bfloat16)

    @pl.when(step < 4)
    def _():
        sib_ref[0] = gated

    @pl.when(step >= 4)
    def _():
        own_ref[0] = gated


def attend_columns(place, normed_ref, w_ref, b0, b1, b2, b3, sib_ref, own_ref, wide_ref, out_ref):
    step = pl.program_id(0)

    @pl.when(step == 0)
    def _():
        load_bias(place, (b0, b1, b2, b3), wide_ref)

    tokens = normed_ref.shape[1]
    bias = wide_ref.reshape(2, tokens, tokens)
    gated = attend(place, normed_ref[0], w_ref, bias, 128)
    chips, two, rows, width, channels = out_ref.shape
    for j in range(width):

        @pl.when(step == j)
        def _():
            out_ref.reshape(tokens, width, channels)[:, j, :] = gated

    @pl.when(step == width - 1)
    def _():
        core = place[0]
        own_ref[...] = out_ref[:, pl.ds(core, 1)][:, 0].astype(jnp.bfloat16)
        sib_ref[...] = out_ref[:, pl.ds(1 - core, 1)][:, 0].astype(jnp.bfloat16)


def finish_rows(own_ref, got_ref, pair_ref, w_ref, one_ref, normed_ref):
    gated = own_ref[0] + got_ref[0]
    branch = jnp.dot(gated, w_ref[...], preferred_element_type=jnp.float32)
    one = (pair_ref[0].astype(jnp.float32) + branch).astype(jnp.bfloat16)
    one_ref[0] = one
    normed = layer_normed(one.astype(jnp.float32))
    chips, _, width, channels = normed_ref.shape
    normed_ref[:, 0] = normed.reshape(chips, width, channels).astype(jnp.bfloat16)


def finish_columns(own_ref, got_ref, w_ref, out_ref):
    chips, rows, width, channels = own_ref.shape
    gated = own_ref[...].astype(jnp.float32) + got_ref[...].astype(jnp.float32)
    gated = gated.reshape(chips * rows * width, channels).astype(jnp.bfloat16)
    branch = jnp.dot(gated, w_ref[...], preferred_element_type=jnp.float32)
    out_ref[...] = branch.reshape(chips, rows, width, channels).astype(jnp.bfloat16)


def add_back(one_ref, back_ref, out_ref):
    chips, _, width, channels = back_ref.shape
    back = back_ref[...].astype(jnp.float32).reshape(chips * width, channels)
    out_ref[0] = (one_ref[0].astype(jnp.float32) + back).astype(jnp.bfloat16)


def swap(array):
    return lax.ppermute(array, "c", [(0, 1), (1, 0)])


def gather_bias(bias, x_chips):
    group = lax.axis_size("y") * lax.axis_size("z")
    copies = jnp.broadcast_to(bias[None], (group,) + bias.shape)
    piece = lax.all_to_all(copies, ("y", "z"), 0, 0)
    return [piece] + [
        lax.ppermute(piece, "x", [(i, i ^ s) for i in range(x_chips)]) for s in range(1, x_chips)
    ]


def full(shape):
    return pl.BlockSpec(shape, lambda *_: (0,) * len(shape))


def run_attention(columns, place, normed, weights, pieces):
    rows, tokens, channels = normed.shape
    chips = tokens // 8
    bf16 = jnp.bfloat16
    specs = [
        SMEM,
        pl.BlockSpec((1, tokens, channels), lambda s: (s, 0, 0)),
        full(weights.shape),
    ] + [full(p.shape) for p in pieces]
    scratch = [pltpu.VMEM((2, chips // 4, 4, 8, tokens), jnp.float32)]
    if columns:
        shape = (chips, 4, 8, channels)
        out_specs = [full(shape), full(shape)]
        scratch.append(pltpu.VMEM((chips, 2, 4, 8, channels), jnp.float32))
        body = attend_columns
    else:
        shape = (rows // 2, tokens, channels)
        block = (1, tokens, channels)
        out_specs = [
            pl.BlockSpec(block, lambda s: (jnp.minimum(s, 3), 0, 0)),
            pl.BlockSpec(block, lambda s: (jnp.maximum(s - 4, 0), 0, 0)),
        ]
        body = attend_rows
    return pl.pallas_call(
        body,
        grid=(rows,),
        in_specs=specs,
        out_specs=out_specs,
        out_shape=[jax.ShapeDtypeStruct(shape, bf16)] * 2,
        scratch_shapes=scratch,
        compiler_params=params(),
    )(place, normed, weights, *pieces)


def shards(pair, valid, w_query, w_key, w_value, w_gate, w_bias, w_out):
    count, tokens, channels = pair.shape
    bf16 = jnp.bfloat16
    x_chips = lax.axis_size("x")
    chips = tokens // (2 * count)
    core, x = lax.axis_index("c"), lax.axis_index("x")
    place = jnp.stack([core, x, valid[0]] + [x ^ s for s in range(x_chips)]).astype(jnp.int32)
    wb = jnp.pad(jnp.swapaxes(w_bias, 1, 2), ((0, 0), (0, 4), (0, 0)))
    weights = jnp.concatenate([w_query, w_key, w_value, w_gate], axis=2)
    piece = (chips, count, 2 * count, channels)

    normed, bias = pl.pallas_call(
        prepare_rows,
        in_specs=[SMEM] + [pl.BlockSpec(memory_space=pltpu.VMEM)] * 3,
        out_specs=[pl.BlockSpec(memory_space=pltpu.VMEM)] * 2,
        out_shape=[
            jax.ShapeDtypeStruct((2 * count, tokens, channels), bf16),
            jax.ShapeDtypeStruct((4 * count, tokens), bf16),
        ],
        scratch_shapes=[pltpu.VMEM((4 * count, tokens), jnp.float32)],
        compiler_params=params(),
    )(place, swap(pair), pair, wb[0])
    pieces = gather_bias(bias, x_chips)
    for_sib, own = run_attention(False, place, normed, weights[0], pieces)
    row = pl.BlockSpec((1, tokens, channels), lambda s: (s, 0, 0))
    one, normed_one = pl.pallas_call(
        finish_rows,
        grid=(count,),
        in_specs=[row, row, row, full((channels, channels))],
        out_specs=[row, pl.BlockSpec((chips, 1, 2 * count, channels), lambda s: (0, s, 0, 0))],
        out_shape=[
            jax.ShapeDtypeStruct((count, tokens, channels), bf16),
            jax.ShapeDtypeStruct(piece, bf16),
        ],
        compiler_params=params(),
    )(own, swap(for_sib), pair, w_out[0])

    got = lax.all_to_all(normed_one, CHIPS, 0, 0)
    normed, bias = pl.pallas_call(
        prepare_columns,
        in_specs=[SMEM] + [pl.BlockSpec(memory_space=pltpu.VMEM)] * 3,
        out_specs=[pl.BlockSpec(memory_space=pltpu.VMEM)] * 2,
        out_shape=[
            jax.ShapeDtypeStruct((2 * count, tokens, channels), bf16),
            jax.ShapeDtypeStruct((4 * count, tokens), bf16),
        ],
        scratch_shapes=[
            pltpu.VMEM((4 * count, tokens), jnp.float32),
            pltpu.VMEM((chips, 2, count, 2 * count, channels), jnp.float32),
        ],
        compiler_params=params(),
    )(place, got, swap(got), wb[1])
    pieces = gather_bias(bias, x_chips)
    for_sib, own = run_attention(True, place, normed, weights[1], pieces)
    branch = pl.pallas_call(
        finish_columns,
        in_specs=[pl.BlockSpec(memory_space=pltpu.VMEM)] * 3,
        out_specs=pl.BlockSpec(memory_space=pltpu.VMEM),
        out_shape=jax.ShapeDtypeStruct(piece, bf16),
        compiler_params=params(),
    )(own, swap(for_sib), w_out[1])
    back = lax.all_to_all(branch, CHIPS, 0, 0)
    return pl.pallas_call(
        add_back,
        grid=(count,),
        in_specs=[row, pl.BlockSpec((chips, 1, 2 * count, channels), lambda s: (0, s, 0, 0))],
        out_specs=row,
        out_shape=jax.ShapeDtypeStruct((count, tokens, channels), bf16),
        compiler_params=params(),
    )(one, back)


def solution(mesh):
    fine = Mesh(mesh.devices.reshape(2, 8, 4, 2, 2), ("y", "z", "x", "c", "dp"))
    held = P(("dp", "y", "z", "x", "c"), None, None)
    return jax.shard_map(
        shards,
        mesh=fine,
        in_specs=(held, P("dp"), P(), P(), P(), P(), P(), P()),
        out_specs=held,
        check_vma=False,
    )
```

```python
import functools
import math

import jax
import jax.numpy as jnp
from jax import lax
from jax.experimental import pallas as pl
from jax.experimental.pallas import tpu as pltpu
from jax.sharding import Mesh, PartitionSpec as P

HEAD_DIM = 32
EPSILON = 1e-05
MASKED = -1000000000.0
VMEM_LIMIT = 48 * 1024 * 1024

X, YZ, ROWS = 4, 16, 8
QUARTER = YZ * ROWS

SMEM = pl.BlockSpec(memory_space=pltpu.SMEM)
VMEM = pl.BlockSpec(memory_space=pltpu.VMEM)
ANY = pl.BlockSpec(memory_space=pl.ANY)

CORE, VALID, SPOT, FIRST_ROW = 0, 2, 3, 7


def params():
    return pltpu.CompilerParams(vmem_limit_bytes=VMEM_LIMIT)


def cost(flops, nbytes, exps=0):
    return pl.CostEstimate(flops=flops, bytes_accessed=nbytes, transcendentals=exps)


def inner_order(rows):
    parts = rows.reshape(YZ, X, ROWS, rows.shape[-1])
    return jnp.concatenate([parts[:, x].reshape(QUARTER, -1) for x in range(X)], axis=0)


def outer_order(rows):
    parts = rows.reshape(X, YZ, ROWS, rows.shape[-1])
    return jnp.stack([parts[x] for x in range(X)], axis=1).reshape(rows.shape)


def layer_normed(wide):
    center = jnp.mean(wide, axis=-1, keepdims=True)
    moved = wide - center
    spread = jnp.mean(jnp.square(moved), axis=-1, keepdims=True)
    return moved * lax.rsqrt(spread + EPSILON)


def bias_rows(wb, normed):
    return lax.dot_general(
        wb, normed, (((1,), (1,)), ((), ())), preferred_element_type=jnp.float32
    )


def prepare_rows(place, sib_ref, own_ref, wb_ref, normed_ref, bias_ref, rows_ref):
    core = place[CORE]
    first = core == 0
    count = own_ref.shape[0]
    for half, (ref, at) in enumerate(((sib_ref, 1 - core), (own_ref, core))):
        for r in range(count):
            wide = inner_order(ref[r].astype(jnp.float32))
            normed = layer_normed(wide).astype(jnp.bfloat16)
            normed_ref[half * count + r] = normed
            four = bias_rows(wb_ref[...], normed)
            spot = at * count + r
            rows_ref[pl.ds(spot, 1), :] = jnp.where(first, four[0:1], four[2:3])
            rows_ref[pl.ds(ROWS + spot, 1), :] = jnp.where(first, four[1:2], four[3:4])
    lane = lax.broadcasted_iota(jnp.int32, bias_ref.shape, 1)
    x, rest = lane // QUARTER, lane % QUARTER
    token = ((rest // ROWS) * X + x) * ROWS + rest % ROWS
    bias_ref[...] = jnp.where(token < place[VALID], rows_ref[...], MASKED).astype(jnp.bfloat16)


def project(core, normed, w_ref):
    tokens, channels = normed.shape
    projected = jnp.dot(normed, w_ref[...], preferred_element_type=jnp.float32)
    query = (projected[:, :channels] * (1.0 / math.sqrt(HEAD_DIM))).astype(jnp.bfloat16)
    key_t = projected[:, channels : 2 * channels].astype(jnp.bfloat16).T
    half = lax.broadcasted_iota(jnp.int32, (tokens, channels), 1) // (2 * HEAD_DIM)
    value = jnp.where(half == core, projected[:, 2 * channels : 3 * channels], 1.0)
    gate = jax.nn.sigmoid(projected[:, 3 * channels :])
    return query, key_t, value.astype(jnp.bfloat16), gate


def project_rows(place, normed_ref, w_ref, query_ref, key_ref, value_ref, gate_ref):
    for r in range(normed_ref.shape[0]):
        query, key_t, value, gate = project(place[CORE], normed_ref[r], w_ref)
        query_ref[r], key_ref[r], value_ref[r], gate_ref[r] = query, key_t, value, gate


def attend(core, units):
    count, channels = units[0][0].shape
    head = lax.broadcasted_iota(jnp.int32, (count, channels), 1) // HEAD_DIM
    mine = head // 2 == core

    def scores(unit):
        query, key_t = unit[0], unit[1]
        zero = jnp.zeros_like(query)
        both = [jnp.where(head == 2 * core + h, query, zero) for h in range(2)]
        return jnp.dot(
            jnp.concatenate(both, axis=0), key_t, preferred_element_type=jnp.float32
        )

    def finish(unit, weight):
        _, _, _, value, gate, put = unit
        out = jnp.dot(weight, value, preferred_element_type=jnp.float32)
        total = jnp.where(head % 2 == 0, out[:count], out[count:])
        sums = pltpu.roll(total, channels // 2, 1)
        put(jnp.where(mine, gate * total / sums, 0.0))

    pending = None
    following = scores(units[0])
    for i, unit in enumerate(units):
        score = following
        if i + 1 < len(units):
            following = scores(units[i + 1])
        score = score + unit[2]().reshape(score.shape)
        highest = jnp.max(score, axis=-1, keepdims=True)
        weight = jnp.exp(score - highest).astype(jnp.bfloat16)
        if pending is not None:
            finish(*pending)
        pending = (unit, weight)
    finish(*pending)


def attend_quarter(count, place, *refs):
    query_ref, key_ref, value_ref, gate_ref = refs[:4]
    pieces = refs[4 : 4 + count]
    sib_ref, own_ref, wide_ref = refs[-3:]
    for step, ref in enumerate(pieces):

        @pl.when(pl.program_id(0) == step)
        def _():
            wide = ref[...].astype(jnp.float32)
            for h in range(2):
                wide_ref[h] = wide[:, h * ROWS : (h + 1) * ROWS].reshape(wide_ref.shape[1:])

    units = []
    for r in range(ROWS):
        out_ref, at = (sib_ref, r) if r < ROWS // 2 else (own_ref, r - ROWS // 2)

        def put(value, out_ref=out_ref, at=at):
            out_ref[at] = value.astype(jnp.bfloat16)

        units.append(
            (query_ref[r], key_ref[r], lambda: wide_ref[...], value_ref[r], gate_ref[r], put)
        )
    attend(place[CORE], units)


def attend_rows(place, projected, steps, pieces, outs):
    query, key_t, value, gate = projected
    rows, tokens, channels = query.shape
    first, stride = SPOT + steps[0], (steps[-1] - steps[0]) // max(len(steps) - 1, 1)
    quarter = lambda s, place: (0, place[first + stride * s], 0)
    whole = lambda s, place: (0, 0, 0)
    half = pl.BlockSpec((rows // 2, QUARTER, channels), quarter)
    shape = jax.ShapeDtypeStruct((rows // 2, tokens, channels), jnp.bfloat16)
    operands = [place, query, key_t, value, gate] + list(pieces)
    specs = [
        pl.BlockSpec((rows, QUARTER, channels), quarter),
        pl.BlockSpec(key_t.shape, whole),
        pl.BlockSpec(value.shape, whole),
        pl.BlockSpec((rows, QUARTER, channels), quarter),
    ] + [pl.BlockSpec(p.shape, whole) for p in pieces]
    aliases = {}
    if outs is not None:
        aliases = {len(operands) + i: i for i in range(2)}
        operands += list(outs)
        specs += [ANY, ANY]
    units = len(steps) * rows * 2
    return pl.pallas_call(
        functools.partial(attend_quarter, len(steps)),
        grid_spec=pltpu.PrefetchScalarGridSpec(
            num_scalar_prefetch=1,
            grid=(len(steps),),
            in_specs=specs,
            out_specs=[half, half],
            scratch_shapes=[pltpu.VMEM((2, QUARTER, tokens), jnp.float32)],
        ),
        out_shape=[shape, shape],
        input_output_aliases=aliases,
        compiler_params=params(),
        cost_estimate=cost(
            units * 4 * QUARTER * tokens * channels, 4 << 20, units * QUARTER * tokens
        ),
    )(*operands)


def finish_rows(place, own_ref, got_ref, pair_ref, w_ref, wb_ref, one_ref, normed_ref, mine_ref, other_ref, rows_ref):
    core = place[CORE]
    first = core == 0
    chips, count, width, channels = normed_ref.shape
    for r in range(count):
        gated = own_ref[r] + got_ref[r]
        branch = jnp.dot(gated, w_ref[...], preferred_element_type=jnp.float32)
        one = (inner_order(pair_ref[r].astype(jnp.float32)) + branch).astype(jnp.bfloat16)
        one_ref[r] = one
        normed = layer_normed(one.astype(jnp.float32))
        normed_ref[:, r] = normed.reshape(chips, width, channels).astype(jnp.bfloat16)
        four = bias_rows(wb_ref[...], normed.astype(jnp.bfloat16))
        four = jnp.where(place[FIRST_ROW] + r < place[VALID], four, MASKED)
        for h in range(2):
            rows_ref[0, pl.ds(h * count + r, 1), :] = jnp.where(
                first, four[h : h + 1], four[2 + h : 3 + h]
            )
            rows_ref[1, pl.ds(h * count + r, 1), :] = jnp.where(
                first, four[2 + h : 3 + h], four[h : h + 1]
            )
    mine_ref[...] = rows_ref[0].astype(jnp.bfloat16)
    other_ref[...] = rows_ref[1].astype(jnp.bfloat16)


def attend_columns(place, own_in, sib_in, w_ref, b0, b1, b2, b3, sib_ref, own_ref, wide_ref, cols_ref, normed_ref, gated_ref):
    step = pl.program_id(0)
    core = place[CORE]
    chips, count, width, channels = own_in.shape
    tokens = chips * 2 * count

    @pl.when(step == 0)
    def _():
        for ref, at in ((own_in, core), (sib_in, 1 - core)):
            cols_ref[:, pl.ds(at, 1)] = ref[...].astype(jnp.float32)[:, None]
        flat = cols_ref.reshape(tokens, width, channels)
        for j in range(width):
            normed_ref[j] = flat[:, j, :].astype(jnp.bfloat16)
        for s, ref in enumerate((b0, b1, b2, b3)):
            at = pl.multiple_of(place[SPOT + s] * QUARTER, QUARTER)
            wide = ref[...].astype(jnp.float32)
            for h in range(2):
                keyed = wide[:, h * ROWS : (h + 1) * ROWS].reshape(QUARTER, tokens)
                wide_ref[h, :, pl.ds(at, QUARTER)] = keyed.T

    chunk = tokens // 2
    units = []
    for j in range(width // 2):
        column = step * (width // 2) + j
        query, key_t, value, gate = project(core, normed_ref[column], w_ref)
        for at in range(0, tokens, chunk):

            def put(value, column=column, at=at):
                gated_ref[pl.ds(column, 1), at : at + chunk, :] = value[None]

            def bias(at=at):
                return wide_ref[:, at : at + chunk, :]

            units.append(
                (query[at : at + chunk], key_t, bias, value, gate[at : at + chunk], put)
            )
    attend(core, units)

    @pl.when(step == 1)
    def _():
        flat = cols_ref.reshape(tokens, width, channels)
        for j in range(width):
            flat[:, j, :] = gated_ref[j]
        own_ref[...] = cols_ref[:, pl.ds(core, 1)][:, 0].astype(jnp.bfloat16)
        sib_ref[...] = cols_ref[:, pl.ds(1 - core, 1)][:, 0].astype(jnp.bfloat16)


def finish_columns(own_ref, got_ref, w_ref, out_ref):
    chips, rows, width, channels = own_ref.shape
    gated = own_ref[...].astype(jnp.float32) + got_ref[...].astype(jnp.float32)
    gated = gated.reshape(chips * rows * width, channels).astype(jnp.bfloat16)
    branch = jnp.dot(gated, w_ref[...], preferred_element_type=jnp.float32)
    out_ref[...] = branch.reshape(chips, rows, width, channels).astype(jnp.bfloat16)


def add_back(one_ref, back_ref, out_ref):
    chips, count, width, channels = back_ref.shape
    for r in range(count):
        back = back_ref[:, r].astype(jnp.float32).reshape(chips * width, channels)
        total = one_ref[r].astype(jnp.float32) + back
        out_ref[r] = outer_order(total).astype(jnp.bfloat16)


def swap(array):
    return lax.ppermute(array, "c", [(0, 1), (1, 0)])


def gather_bias(bias):
    copies = jnp.broadcast_to(bias[None], (YZ,) + bias.shape)
    piece = lax.all_to_all(copies, ("y", "z"), 0, 0)
    moved = {s: lax.ppermute(piece, "x", [(i, i ^ s) for i in range(X)]) for s in (1, 3, 2)}
    return [piece, moved[1], moved[2], moved[3]]


def struct(shape, kind=jnp.bfloat16):
    return jax.ShapeDtypeStruct(shape, kind)


def shards(pair, valid, w_query, w_key, w_value, w_gate, w_bias, w_out):
    count, tokens, channels = pair.shape
    core, x = lax.axis_index("c"), lax.axis_index("x")
    chip = lax.axis_index("y") * lax.axis_size("z") + lax.axis_index("z")
    first_row = (chip * X + x) * ROWS + core * count
    place = jnp.stack([core, x, valid[0]] + [x ^ s for s in range(X)] + [first_row])
    place = place.astype(jnp.int32)
    wb = jnp.pad(jnp.swapaxes(w_bias, 1, 2), ((0, 0), (0, 4), (0, 0)))
    weights = jnp.concatenate([w_query, w_key, w_value, w_gate], axis=2)
    chips = X * YZ
    piece = (chips, count, ROWS, channels)
    rows = (ROWS, tokens, channels)

    normed, bias = pl.pallas_call(
        prepare_rows,
        in_specs=[SMEM, VMEM, VMEM, VMEM],
        out_specs=[VMEM, VMEM],
        out_shape=[struct(rows), struct((2 * ROWS, tokens))],
        scratch_shapes=[pltpu.VMEM((2 * ROWS, tokens), jnp.float32)],
        compiler_params=params(),
        cost_estimate=cost(1 << 25, 2 << 20),
    )(place, swap(pair), pair, wb[0])
    pieces = gather_bias(bias)
    block = pl.BlockSpec((ROWS // 2, tokens, channels), lambda s: (s, 0, 0))
    block_t = pl.BlockSpec((ROWS // 2, channels, tokens), lambda s: (s, 0, 0))
    projected = pl.pallas_call(
        project_rows,
        grid=(2,),
        in_specs=[SMEM, block, pl.BlockSpec((channels, 4 * channels), lambda s: (0, 0))],
        out_specs=[block, block_t, block, block],
        out_shape=[
            struct(rows),
            struct((ROWS, channels, tokens)),
            struct(rows),
            struct(rows, jnp.float32),
        ],
        compiler_params=params(),
        cost_estimate=cost(8 * ROWS * tokens * channels * channels, 6 << 20),
    )(place, normed, weights[0])
    outs = attend_rows(place, projected, (0,), pieces[:1], None)
    outs = attend_rows(place, projected, (1, 3), [pieces[1], pieces[3]], outs)
    for_sib, own = attend_rows(place, projected, (2,), pieces[2:3], outs)
    one, normed_one, mine, other = pl.pallas_call(
        finish_rows,
        in_specs=[SMEM] + [VMEM] * 5,
        out_specs=[VMEM] * 4,
        out_shape=[
            struct((count, tokens, channels)),
            struct(piece),
            struct((2 * count, tokens)),
            struct((2 * count, tokens)),
        ],
        scratch_shapes=[pltpu.VMEM((2, 2 * count, tokens), jnp.float32)],
        compiler_params=params(),
        cost_estimate=cost(1 << 27, 3 << 20),
    )(place, own, swap(for_sib), pair, w_out[0], wb[1])

    got_bias = swap(other)
    mine, got_bias = mine.reshape(2, count, tokens), got_bias.reshape(2, count, tokens)
    low, high = jnp.where(core == 0, mine, got_bias), jnp.where(core == 0, got_bias, mine)
    bias = jnp.stack([low, high], axis=1).reshape(2 * ROWS, tokens)
    pieces = gather_bias(bias)
    got = lax.all_to_all(normed_one, ("x", "y", "z"), 0, 0)
    for_sib, own = pl.pallas_call(
        attend_columns,
        grid=(2,),
        in_specs=[SMEM]
        + [pl.BlockSpec(piece, lambda s: (0, 0, 0, 0))] * 2
        + [pl.BlockSpec((channels, 4 * channels), lambda s: (0, 0))]
        + [pl.BlockSpec((YZ, 2 * ROWS, tokens), lambda s: (0, 0, 0))] * X,
        out_specs=[pl.BlockSpec(piece, lambda s: (0, 0, 0, 0))] * 2,
        out_shape=[struct(piece)] * 2,
        scratch_shapes=[
            pltpu.VMEM((2, tokens, tokens), jnp.float32),
            pltpu.VMEM((chips, 2, count, ROWS, channels), jnp.float32),
            pltpu.VMEM(rows, jnp.bfloat16),
            pltpu.VMEM(rows, jnp.float32),
        ],
        compiler_params=params(),
        cost_estimate=cost(1 << 33, 4 << 20, 1 << 22),
    )(place, got, swap(got), weights[1], *pieces)
    branch = pl.pallas_call(
        finish_columns,
        in_specs=[VMEM] * 3,
        out_specs=VMEM,
        out_shape=struct(piece),
        compiler_params=params(),
    )(own, swap(for_sib), w_out[1])
    back = lax.all_to_all(branch, ("x", "y", "z"), 0, 0)
    return pl.pallas_call(
        add_back,
        in_specs=[VMEM, VMEM],
        out_specs=VMEM,
        out_shape=struct((count, tokens, channels)),
        compiler_params=params(),
    )(one, back)


def solution(mesh):
    fine = Mesh(mesh.devices.reshape(2, 8, 4, 2, 2), ("y", "z", "x", "c", "dp"))
    held = P(("dp", "y", "z", "x", "c"), None, None)
    return jax.shard_map(
        shards,
        mesh=fine,
        in_specs=(held, P("dp"), P(), P(), P(), P(), P(), P()),
        out_specs=held,
        check_vma=False,
    )
```

```python
import functools
import math

import jax
import jax.numpy as jnp
from jax import lax
from jax.experimental import pallas as pl
from jax.experimental.pallas import tpu as pltpu
from jax.sharding import Mesh, PartitionSpec as P

HEAD_DIM = 32
EPSILON = 1e-05
MASKED = -1000000000.0

X, YZ, ROWS = 4, 16, 8
QUARTER = YZ * ROWS

SMEM = pl.BlockSpec(memory_space=pltpu.SMEM)
VMEM = pl.BlockSpec(memory_space=pltpu.VMEM)

CORE, VALID, SPOT, FIRST_ROW = 0, 2, 3, 7


def params(mebibytes=12):
    return pltpu.CompilerParams(vmem_limit_bytes=mebibytes * 1024 * 1024)


def cost(flops, nbytes, exps=0):
    return pl.CostEstimate(flops=flops, bytes_accessed=nbytes, transcendentals=exps)


def inner_order(rows):
    parts = rows.reshape(YZ, X, ROWS, rows.shape[-1])
    return jnp.concatenate([parts[:, x].reshape(QUARTER, -1) for x in range(X)], axis=0)


def outer_order(rows):
    parts = rows.reshape(X, YZ, ROWS, rows.shape[-1])
    return jnp.stack([parts[x] for x in range(X)], axis=1).reshape(rows.shape)


def layer_normed(wide):
    center = jnp.mean(wide, axis=-1, keepdims=True)
    moved = wide - center
    spread = jnp.mean(jnp.square(moved), axis=-1, keepdims=True)
    return moved * lax.rsqrt(spread + EPSILON)


def bias_rows(wb_ref, step, normed, r, count, masked, rows_ref):
    four = lax.dot_general(
        wb_ref[step], normed, (((1,), (1,)), ((), ())), preferred_element_type=jnp.float32
    )
    four = jnp.where(masked, MASKED, four)
    for h in range(four.shape[0]):
        rows_ref[h * count + r : h * count + r + 1, :] = four[h : h + 1]


def prepare_rows(place, pair_ref, wb_ref, normed_ref, mine_ref, other_ref, rows_ref):
    count, tokens, _ = pair_ref.shape
    lane = lax.broadcasted_iota(jnp.int32, (1, tokens), 1)
    x, rest = lane // QUARTER, lane % QUARTER
    token = ((rest // ROWS) * X + x) * ROWS + rest % ROWS
    masked = token >= place[VALID]
    for r in range(count):
        wide = inner_order(pair_ref[r].astype(jnp.float32))
        normed = layer_normed(wide).astype(jnp.bfloat16)
        normed_ref[r] = normed
        bias_rows(wb_ref, 0, normed, r, count, masked, rows_ref)
    low, high = rows_ref[: 2 * count], rows_ref[2 * count :]
    first = place[CORE] == 0
    mine_ref[...] = jnp.where(first, low, high).astype(jnp.bfloat16)
    other_ref[...] = jnp.where(first, high, low).astype(jnp.bfloat16)


def project(core, normed, weights):
    tokens, channels = normed.shape
    projected = jnp.dot(normed, weights, preferred_element_type=jnp.float32)
    query = (projected[:, :channels] * (1.0 / math.sqrt(HEAD_DIM))).astype(jnp.bfloat16)
    key_t = projected[:, channels : 2 * channels].astype(jnp.bfloat16).T
    half = lax.broadcasted_iota(jnp.int32, (tokens, channels), 1) // (2 * HEAD_DIM)
    value = jnp.where(half == core, projected[:, 2 * channels : 3 * channels], 1.0)
    gate = jax.nn.sigmoid(projected[:, 3 * channels :])
    return query, key_t, value.astype(jnp.bfloat16), gate


def project_rows(place, sib_ref, own_ref, *refs):
    w_refs, (query_ref, key_ref, value_ref, gate_ref, next_ref) = refs[:4], refs[4:]
    weights = jnp.concatenate([ref[0] for ref in w_refs], axis=1)
    next_ref[...] = jnp.concatenate([ref[1] for ref in w_refs], axis=1)
    for r in range(ROWS):
        normed = sib_ref[r] if r < ROWS // 2 else own_ref[r - ROWS // 2]
        query, key_t, value, gate = project(place[CORE], normed, weights)
        query_ref[r], key_ref[r], value_ref[r], gate_ref[r] = query, key_t, value, gate


def project_columns(place, own_in, sib_in, w_ref, query_ref, key_ref, value_ref, gate_ref, cols_ref):
    core = place[CORE]
    chips, _, count, width, channels = cols_ref.shape
    for ref, at in ((own_in, core), (sib_in, 1 - core)):
        part = ref[:, : count * width, :].astype(jnp.float32)
        cols_ref[:, pl.ds(at, 1)] = part.reshape(chips, 1, count, width, channels)
    flat = cols_ref.reshape(chips * 2 * count, width, channels)
    for j in range(width):
        normed = flat[:, j, :].astype(jnp.bfloat16)
        query, key_t, value, gate = project(core, normed, w_ref[...])
        query_ref[j], key_ref[j], value_ref[j], gate_ref[j] = query, key_t, value, gate


def turn_bias(place, own_in, sib_in, out_ref, keyed_ref):
    first = place[CORE] == 0
    chips, width, _ = keyed_ref.shape[1:]
    count = width // 2
    parts = []
    for ref in (own_in, sib_in):
        rows = ref[:, count * width :, :].astype(jnp.float32)
        parts.append(jnp.where(first, rows[:, : 2 * count], rows[:, 2 * count :]))
    own, sib = parts
    low, high = jnp.where(first, own, sib), jnp.where(first, sib, own)
    for h in range(2):
        keyed_ref[h, :, :count, :] = low[:, h * count : (h + 1) * count]
        keyed_ref[h, :, count:, :] = high[:, h * count : (h + 1) * count]
        keyed = keyed_ref[h].reshape(chips * width, -1)
        out_ref[h] = keyed.T.astype(jnp.bfloat16)


def attend(core, units, count, channels):
    head = lax.broadcasted_iota(jnp.int32, (count, channels), 1) // HEAD_DIM
    mine = head // 2 == core

    def scores(unit):
        query, key_t = unit[0](), unit[1]()
        zero = jnp.zeros_like(query)
        both = [jnp.where(head == 2 * core + h, query, zero) for h in range(2)]
        return jnp.dot(
            jnp.concatenate(both, axis=0), key_t, preferred_element_type=jnp.float32
        )

    def finish(unit, weight):
        _, _, _, value, gate, put = unit
        out = jnp.dot(weight, value(), preferred_element_type=jnp.float32)
        total = jnp.where(head % 2 == 0, out[:count], out[count:])
        sums = pltpu.roll(total, channels // 2, 1)
        put(jnp.where(mine, gate() * total / sums, 0.0))

    pending = None
    following = scores(units[0])
    for i, unit in enumerate(units):
        score = following
        if i + 1 < len(units):
            following = scores(units[i + 1])
        score = score + unit[2]().reshape(score.shape)
        highest = jnp.max(score, axis=-1, keepdims=True)
        weight = jnp.exp(score - highest).astype(jnp.bfloat16)
        if pending is not None:
            finish(*pending)
        pending = (unit, weight)
    finish(*pending)


def attend_quarters(steps, columns, place, *refs):
    core = place[CORE]
    query_ref, key_ref, value_ref, gate_ref = refs[:4]
    pieces = refs[4 : 4 + len(steps)]
    sib_ref, own_ref, wide_ref = refs[-4:-1] if columns else refs[-3:]
    out_ref = refs[-1]
    units = []
    for i, (s, piece_ref) in enumerate(zip(steps, pieces)):
        wide = piece_ref[...].astype(jnp.float32)
        for h in range(2):
            rows = wide[h] if columns else wide[:, h * ROWS : (h + 1) * ROWS]
            wide_ref[i, h] = rows.reshape(wide_ref.shape[2:])
        span = pl.ds(pl.multiple_of(place[SPOT + s] * QUARTER, QUARTER), QUARTER)
        for r in range(ROWS):

            def put(value, i=i, r=r, span=span):
                if columns:
                    out_ref.reshape(len(steps), QUARTER, ROWS, -1)[i, :, r, :] = value
                elif r < ROWS // 2:
                    sib_ref[r, span, :] = value.astype(jnp.bfloat16)
                else:
                    own_ref[r - ROWS // 2, span, :] = value.astype(jnp.bfloat16)

            units.append(
                (
                    lambda r=r, span=span: query_ref[r, span, :],
                    lambda r=r: key_ref[r],
                    lambda i=i: wide_ref[i],
                    lambda r=r: value_ref[r],
                    lambda r=r, span=span: gate_ref[r, span, :],
                    put,
                )
            )
    attend(core, units, QUARTER, query_ref.shape[-1])
    if columns:
        for i, s in enumerate(steps):
            chips = pl.ds(place[SPOT + s] * YZ, YZ)
            for ref, at in ((own_ref, core), (sib_ref, 1 - core)):
                ref[chips] = out_ref[i, :, pl.ds(at, 1)][:, 0].astype(jnp.bfloat16)


def attend_some(steps, columns, place, projected, pieces, outs):
    rows, tokens, channels = projected[0].shape
    count = rows // 2
    scratch = [pltpu.VMEM((len(steps), 2, QUARTER, tokens), jnp.float32)]
    if columns:
        shape = struct((X * YZ, count, rows, channels))
        scratch.append(pltpu.VMEM((len(steps), YZ, 2, count, rows, channels), jnp.float32))
    else:
        shape = struct((count, tokens, channels))
    operands = [place, *projected, *pieces]
    aliases = {}
    if outs is not None:
        aliases = {len(operands) + i: i for i in range(2)}
        operands += list(outs)
    units = len(steps) * rows * 2
    return pl.pallas_call(
        functools.partial(attend_quarters, steps, columns),
        in_specs=[SMEM] + [VMEM] * (len(operands) - 1),
        out_specs=[VMEM, VMEM],
        scratch_shapes=scratch,
        out_shape=[shape, shape],
        input_output_aliases=aliases,
        compiler_params=params(16),
        cost_estimate=cost(
            units * 4 * QUARTER * tokens * channels, 4 << 20, units * QUARTER * tokens
        ),
    )(*operands)


def attend_all(columns, place, projected, piece):
    moved = {s: lax.ppermute(piece, "x", [(i, i ^ s) for i in range(X)]) for s in (1, 3, 2)}
    outs = attend_some((0,), columns, place, projected, [piece], None)
    outs = attend_some((1, 3), columns, place, projected, [moved[1], moved[3]], outs)
    return attend_some((2,), columns, place, projected, [moved[2]], outs)


def finish_rows(place, own_ref, got_ref, pair_ref, w_ref, wb_ref, one_ref, sent_ref, rows_ref, wide_ref):
    count, tokens, channels = own_ref.shape
    chips = sent_ref.shape[0]
    for r in range(count):
        gated = own_ref[r] + got_ref[r]
        branch = jnp.dot(gated, w_ref[0], preferred_element_type=jnp.float32)
        one = (inner_order(pair_ref[r].astype(jnp.float32)) + branch).astype(jnp.bfloat16)
        one_ref[r] = one
        normed = layer_normed(one.astype(jnp.float32))
        wide_ref[:, r * ROWS : (r + 1) * ROWS] = normed.reshape(chips, ROWS, channels)
        masked = place[FIRST_ROW] + r >= place[VALID]
        bias_rows(wb_ref, 1, normed.astype(jnp.bfloat16), r, count, masked, rows_ref)
    sent_ref[:, : count * ROWS] = wide_ref[...].astype(jnp.bfloat16)
    for x in range(X):
        quarter = rows_ref[:, x * QUARTER : (x + 1) * QUARTER].astype(jnp.bfloat16)
        sent_ref[x * YZ : (x + 1) * YZ, count * ROWS :] = jnp.broadcast_to(
            quarter[None], (YZ,) + quarter.shape
        )


def finish_columns(own_ref, got_ref, w_ref, out_ref):
    chips, rows, width, channels = own_ref.shape
    gated = own_ref[...].astype(jnp.float32) + got_ref[...].astype(jnp.float32)
    gated = gated.reshape(chips * rows * width, channels).astype(jnp.bfloat16)
    branch = jnp.dot(gated, w_ref[1], preferred_element_type=jnp.float32)
    out_ref[...] = branch.reshape(chips, rows, width, channels).astype(jnp.bfloat16)


def add_back(one_ref, back_ref, out_ref):
    chips, count, width, channels = back_ref.shape
    for r in range(count):
        back = back_ref[:, r].astype(jnp.float32).reshape(chips * width, channels)
        total = one_ref[r].astype(jnp.float32) + back
        out_ref[r] = outer_order(total).astype(jnp.bfloat16)


def swap(array):
    return lax.ppermute(array, "c", [(0, 1), (1, 0)])


def spread_bias(core, mine, other):
    got = swap(other)
    rows, tokens = mine.shape
    mine, got = (a.reshape(2, rows // 2, tokens) for a in (mine, got))
    low, high = jnp.where(core == 0, mine, got), jnp.where(core == 0, got, mine)
    bias = jnp.stack([low, high], axis=1).reshape(2 * rows, tokens)
    return lax.all_to_all(jnp.broadcast_to(bias[None], (YZ,) + bias.shape), ("y", "z"), 0, 0)


def whole(shape):
    return pl.BlockSpec(shape, lambda s: (0,) * len(shape))


def struct(shape, kind=jnp.bfloat16):
    return jax.ShapeDtypeStruct(shape, kind)


def shards(pair, valid, w_query, w_key, w_value, w_gate, w_bias, w_out):
    count, tokens, channels = pair.shape
    core, x = lax.axis_index("c"), lax.axis_index("x")
    chip = lax.axis_index("y") * lax.axis_size("z") + lax.axis_index("z")
    first_row = (chip * X + x) * ROWS + core * count
    place = jnp.stack([core, x, valid[0]] + [x ^ s for s in range(X)] + [first_row])
    place = place.astype(jnp.int32)
    wb = jnp.swapaxes(w_bias, 1, 2)
    weights = [w_query, w_key, w_value, w_gate]
    piece = (X * YZ, count, ROWS, channels)
    rows = (ROWS, tokens, channels)
    held = (count, tokens, channels)
    half = struct((ROWS, tokens))
    bias_scratch = pltpu.VMEM((4 * count, tokens), jnp.float32)
    projections = [
        struct(rows),
        struct((ROWS, channels, tokens)),
        struct(rows),
        struct(rows, jnp.float32),
    ]

    normed, mine, other = pl.pallas_call(
        prepare_rows,
        grid=(1,),
        in_specs=[SMEM, whole(pair.shape), whole(wb.shape)],
        out_specs=[VMEM] * 3,
        out_shape=[struct(held), half, half],
        scratch_shapes=[bias_scratch],
        compiler_params=params(),
        cost_estimate=cost(1 << 25, 2 << 20),
    )(place, pair, wb)
    gathered = spread_bias(core, mine, other)
    *projected, next_weights = pl.pallas_call(
        project_rows,
        in_specs=[SMEM] + [VMEM] * 6,
        out_specs=[VMEM] * 5,
        out_shape=projections + [struct((channels, 4 * channels))],
        compiler_params=params(),
        cost_estimate=cost(8 * ROWS * tokens * channels * channels, 6 << 20),
    )(place, swap(normed), normed, *weights)
    gathered, *projected = lax.optimization_barrier((gathered, *projected))
    for_sib, own = attend_all(False, place, projected, gathered)
    message = (X * YZ, count * ROWS + 4 * count, channels)
    one, sent = pl.pallas_call(
        finish_rows,
        in_specs=[SMEM] + [VMEM] * 5,
        out_specs=[VMEM] * 2,
        out_shape=[struct(held), struct(message)],
        scratch_shapes=[
            bias_scratch,
            pltpu.VMEM((X * YZ, count * ROWS, channels), jnp.float32),
        ],
        compiler_params=params(),
        cost_estimate=cost(1 << 27, 3 << 20),
    )(place, own, swap(for_sib), pair, w_out, wb)

    got = lax.all_to_all(sent, ("x", "y", "z"), 0, 0)
    got_sib = swap(got)
    quarter = pl.pallas_call(
        turn_bias,
        in_specs=[SMEM, VMEM, VMEM],
        out_specs=VMEM,
        out_shape=struct((2, QUARTER, tokens)),
        scratch_shapes=[pltpu.VMEM((2, X * YZ, ROWS, QUARTER), jnp.float32)],
        compiler_params=params(),
        cost_estimate=cost(1 << 20, 3 << 20),
    )(place, got, got_sib)
    projected = pl.pallas_call(
        project_columns,
        in_specs=[SMEM] + [VMEM] * 3,
        out_specs=[VMEM] * 4,
        out_shape=projections,
        scratch_shapes=[pltpu.VMEM((X * YZ, 2, count, ROWS, channels), jnp.float32)],
        compiler_params=params(),
        cost_estimate=cost(8 * ROWS * tokens * channels * channels, 6 << 20),
    )(place, got, got_sib, next_weights)
    for_sib, own = attend_all(True, place, projected, quarter)
    branch = pl.pallas_call(
        finish_columns,
        in_specs=[VMEM] * 3,
        out_specs=VMEM,
        out_shape=struct(piece),
        compiler_params=params(),
    )(own, swap(for_sib), w_out)
    back = lax.all_to_all(branch, ("x", "y", "z"), 0, 0)
    return pl.pallas_call(
        add_back,
        in_specs=[VMEM, VMEM],
        out_specs=VMEM,
        out_shape=struct(held),
        compiler_params=params(),
    )(one, back)


def solution(mesh):
    fine = Mesh(mesh.devices.reshape(2, 8, 4, 2, 2), ("y", "z", "x", "c", "dp"))
    held = P(("dp", "y", "z", "x", "c"), None, None)
    return jax.shard_map(
        shards,
        mesh=fine,
        in_specs=(held, P("dp"), P(), P(), P(), P(), P(), P()),
        out_specs=held,
        check_vma=False,
    )
```

```python
import functools
import math

import jax
import jax.numpy as jnp
from jax import lax
from jax.experimental import pallas as pl
from jax.experimental.pallas import tpu as pltpu
from jax.sharding import Mesh, PartitionSpec as P

HEAD_DIM = 32
EPSILON = 1e-05
MASKED = -1000000000.0

X, YZ, ROWS = 4, 16, 8
QUARTER = YZ * ROWS

SMEM = pl.BlockSpec(memory_space=pltpu.SMEM)
VMEM = pl.BlockSpec(memory_space=pltpu.VMEM)

HALF = 2 * QUARTER

CORE, UPPER, VALID, SPOT, FIRST_ROW, LOCAL = 0, 1, 2, 3, 7, 9
X_AXES = ("xh", "xl")


def params(mebibytes=12):
    return pltpu.CompilerParams(vmem_limit_bytes=mebibytes * 1024 * 1024)


def cost(flops, nbytes, exps=0):
    return pl.CostEstimate(flops=flops, bytes_accessed=nbytes, transcendentals=exps)


def inner_order(rows):
    return jnp.concatenate(inner_quarters(rows), axis=0)


def inner_quarters(rows):
    parts = rows.reshape(YZ, X, ROWS, rows.shape[-1])
    return [parts[:, x].reshape(QUARTER, -1) for x in range(X)]


def outer_order(rows):
    parts = rows.reshape(X, YZ, ROWS, rows.shape[-1])
    return jnp.stack([parts[x] for x in range(X)], axis=1).reshape(rows.shape)


def layer_normed(wide):
    center = jnp.mean(wide, axis=-1, keepdims=True)
    moved = wide - center
    spread = jnp.mean(jnp.square(moved), axis=-1, keepdims=True)
    return moved * lax.rsqrt(spread + EPSILON)


def bias_rows(wb_ref, step, normed, r, count, masked, rows_ref):
    four = lax.dot_general(
        wb_ref[step], normed, (((1,), (1,)), ((), ())), preferred_element_type=jnp.float32
    )
    four = jnp.where(masked, MASKED, four)
    for h in range(four.shape[0]):
        rows_ref[h * count + r : h * count + r + 1, :] = four[h : h + 1]


def prepare_rows(place, pair_ref, wb_ref, normed_ref, mine_ref, other_ref, rows_ref):
    count, tokens, _ = pair_ref.shape
    lane = lax.broadcasted_iota(jnp.int32, (1, tokens), 1)
    x, rest = lane // QUARTER, lane % QUARTER
    token = ((rest // ROWS) * X + x) * ROWS + rest % ROWS
    masked = token >= place[VALID]
    for r in range(count):
        wide = inner_order(pair_ref[r].astype(jnp.float32))
        normed = layer_normed(wide).astype(jnp.bfloat16)
        normed_ref[r] = normed
        bias_rows(wb_ref, 0, normed, r, count, masked, rows_ref)
    low, high = rows_ref[: 2 * count], rows_ref[2 * count :]
    first = place[CORE] == 0
    mine_ref[...] = jnp.where(first, low, high).astype(jnp.bfloat16)
    other_ref[...] = jnp.where(first, high, low).astype(jnp.bfloat16)


def prepare_far(far_ref, normed_ref):
    for r in range(far_ref.shape[0]):
        wide = inner_order(far_ref[r].astype(jnp.float32))
        normed_ref[r] = layer_normed(wide).astype(jnp.bfloat16)


def project(core, normed, weights):
    tokens, channels = normed.shape
    projected = jnp.dot(normed, weights, preferred_element_type=jnp.float32)
    query = (projected[:, :channels] * (1.0 / math.sqrt(HEAD_DIM))).astype(jnp.bfloat16)
    key_t = projected[:, channels : 2 * channels].astype(jnp.bfloat16).T
    half = lax.broadcasted_iota(jnp.int32, (tokens, channels), 1) // (2 * HEAD_DIM)
    value = jnp.where(half == core, projected[:, 2 * channels : 3 * channels], 1.0)
    gate = jax.nn.sigmoid(projected[:, 3 * channels :])
    return query, key_t, value.astype(jnp.bfloat16), gate


def pack_weights(wq, wk, wv, wg, first_ref, next_ref):
    for step, ref in enumerate((first_ref, next_ref)):
        ref[...] = jnp.concatenate([w[step] for w in (wq, wk, wv, wg)], axis=1)


def project_rows(place, sib_ref, own_ref, w_ref, query_ref, key_ref, value_ref, gate_ref, done_ref):
    done_ref[...] = jnp.zeros_like(done_ref)
    for r in range(ROWS):
        normed = sib_ref[r] if r < ROWS // 2 else own_ref[r - ROWS // 2]
        query, key_t, value, gate = project(place[CORE], normed, w_ref[...])
        query_ref[r], key_ref[r], value_ref[r], gate_ref[r] = query, key_t, value, gate


def received_quarters(place):
    upper = place[UPPER]
    return [
        (x, far, 2 * (1 - upper if far else upper) + x) for x in range(X // 2) for far in range(2)
    ]


def project_columns(place, own_in, sib_in, w_ref, query_ref, key_ref, value_ref, gate_ref, cols_ref):
    core = place[CORE]
    _, _, _, count, width, channels = cols_ref.shape
    for ref, at in ((own_in, core), (sib_in, 1 - core)):
        part = ref[:, : 2 * count * width, :].astype(jnp.float32)
        part = part.reshape(X // 2, YZ, 2, count, width, channels)
        for x, far, quarter in received_quarters(place):
            cols_ref[pl.ds(quarter, 1), :, pl.ds(at, 1)] = part[x, :, far][None, :, None]
    flat = cols_ref.reshape(X * YZ * 2 * count, width, channels)
    for j in range(width):
        normed = flat[:, j, :].astype(jnp.bfloat16)
        query, key_t, value, gate = project(core, normed, w_ref[...])
        query_ref[j], key_ref[j], value_ref[j], gate_ref[j] = query, key_t, value, gate


def turn_bias(place, own_in, sib_in, out_ref, keyed_ref):
    first = place[CORE] == 0
    _, _, _, width, _ = keyed_ref.shape
    count = width // 2
    parts = []
    for ref in (own_in, sib_in):
        rows = ref[:, 2 * count * width :, :].astype(jnp.float32)
        middle = rows.shape[1] // 2
        parts.append(jnp.where(first, rows[:, :middle], rows[:, middle:]))
    own, sib = parts
    low, high = jnp.where(first, own, sib), jnp.where(first, sib, own)
    for h in range(2):
        for x, far, quarter in received_quarters(place):
            at = (2 * h + far) * count
            for core, part in enumerate((low, high)):
                piece = part[x * YZ : (x + 1) * YZ, at : at + count]
                keyed_ref[h, pl.ds(quarter, 1), :, core * count : (core + 1) * count] = piece[None]
        keyed = keyed_ref[h].reshape(X * YZ * width, -1)
        out_ref[h] = keyed.T.astype(jnp.bfloat16)


def attend(core, units, count, channels):
    head = lax.broadcasted_iota(jnp.int32, (count, channels), 1) // HEAD_DIM
    mine = head // 2 == core

    def scores(unit):
        query, key_t = unit[0](), unit[1]()
        zero = jnp.zeros_like(query)
        both = [jnp.where(head == 2 * core + h, query, zero) for h in range(2)]
        return jnp.dot(
            jnp.concatenate(both, axis=0), key_t, preferred_element_type=jnp.float32
        )

    def finish(unit, weight):
        _, _, _, value, gate, put = unit
        out = jnp.dot(weight, value(), preferred_element_type=jnp.float32)
        total = jnp.where(head % 2 == 0, out[:count], out[count:])
        sums = pltpu.roll(total, channels // 2, 1)
        put(jnp.where(mine, gate() * total / sums, 0.0))

    pending = None
    following = scores(units[0])
    for i, unit in enumerate(units):
        score = following
        if i + 1 < len(units):
            following = scores(units[i + 1])
        score = score + unit[2]().reshape(score.shape)
        highest = jnp.max(score, axis=-1, keepdims=True)
        weight = jnp.exp(score - highest).astype(jnp.bfloat16)
        if pending is not None:
            finish(*pending)
        pending = (unit, weight)
    finish(*pending)


def attend_quarters(steps, columns, place, *refs):
    core = place[CORE]
    groups = 1 if columns else 2
    pieces = refs[4 * groups : 4 * groups + len(steps)]
    sib_ref, own_ref, wide_ref = refs[-4:-1] if columns else refs[-3:]
    out_ref = refs[-1]
    units = []
    for i, (s, piece_ref) in enumerate(zip(steps, pieces)):
        wide = piece_ref[...].astype(jnp.float32)
        for h in range(2):
            rows = wide[h] if columns else wide[:, h * ROWS : (h + 1) * ROWS]
            wide_ref[i, h] = rows.reshape(wide_ref.shape[2:])
        span = pl.ds(pl.multiple_of(place[SPOT + s] * QUARTER, QUARTER), QUARTER)
        for g in range(groups):
            query_ref, key_ref, value_ref, gate_ref = refs[4 * g : 4 * g + 4]
            for r in range(ROWS):

                def put(value, i=i, g=g, r=r, s=s):
                    if columns:
                        out_ref.reshape(len(steps), QUARTER, ROWS, -1)[i, :, r, :] = value
                        return
                    local = pl.ds(pl.multiple_of(place[LOCAL + s] * QUARTER, QUARTER), QUARTER)
                    half = ROWS // 2
                    ref = sib_ref if r < half else own_ref
                    ref[g * half + r % half, local, :] = value.astype(jnp.bfloat16)

                units.append(
                    (
                        lambda ref=query_ref, r=r, span=span: ref[r, span, :],
                        lambda ref=key_ref, r=r: ref[r],
                        lambda i=i: wide_ref[i],
                        lambda ref=value_ref, r=r: ref[r],
                        lambda ref=gate_ref, r=r, span=span: ref[r, span, :],
                        put,
                    )
                )
    attend(core, units, QUARTER, sib_ref.shape[-1])
    if columns:
        for i, s in enumerate(steps):
            chips = pl.ds(place[SPOT + s] * YZ, YZ)
            for ref, at in ((own_ref, core), (sib_ref, 1 - core)):
                ref[chips] = out_ref[i, :, pl.ds(at, 1)][:, 0].astype(jnp.bfloat16)


def attend_some(steps, columns, place, projected, pieces, outs):
    rows, tokens, channels = projected[0].shape
    count = rows // 2
    scratch = [pltpu.VMEM((len(steps), 2, QUARTER, tokens), jnp.float32)]
    if columns:
        shape = struct((X * YZ, count, rows, channels))
        scratch.append(pltpu.VMEM((len(steps), YZ, 2, count, rows, channels), jnp.float32))
    else:
        shape = struct((rows, HALF, channels))
    operands = [place, *projected, *pieces]
    aliases = {}
    if outs is not None:
        aliases = {len(operands) + i: i for i in range(2)}
        operands += list(outs)
    units = len(steps) * rows * 2 * len(projected) // 4
    return pl.pallas_call(
        functools.partial(attend_quarters, steps, columns),
        in_specs=[SMEM] + [VMEM] * (len(operands) - 1),
        out_specs=[VMEM, VMEM],
        scratch_shapes=scratch,
        out_shape=[shape, shape],
        input_output_aliases=aliases,
        compiler_params=params(16),
        cost_estimate=cost(
            units * 4 * QUARTER * tokens * channels, 4 << 20, units * QUARTER * tokens
        ),
    )(*operands)


def along_x(array, s):
    return lax.ppermute(array, X_AXES, [(i, i ^ s) for i in range(X)])


def attend_all(columns, place, projected, piece):
    steps = [(0,), (1, 3), (2,)] if columns else [(0,), (1,)]
    moved = {s: along_x(piece, s) for some in steps[1:] for s in some}
    outs = attend_some(steps[0], columns, place, projected, [piece], None)
    for some in steps[1:]:
        outs = attend_some(some, columns, place, projected, [moved[s] for s in some], outs)
    return outs


def finish_rows(place, own_ref, got_ref, pair_ref, far_ref, w_ref, wb_ref, near_ref, other_ref, sent_ref, rows_ref, wide_ref):
    count, half, channels = near_ref.shape
    chips = sent_ref.shape[0]
    lower = place[UPPER] == 0
    for far, (raw_ref, one_ref) in enumerate(((pair_ref, near_ref), (far_ref, other_ref))):
        for r in range(count):
            at = far * count + r
            gated = own_ref[at] + got_ref[at]
            branch = jnp.dot(gated, w_ref[0], preferred_element_type=jnp.float32)
            q = inner_quarters(raw_ref[r].astype(jnp.float32))
            raw = jnp.concatenate([jnp.where(lower, q[x], q[2 + x]) for x in range(2)], axis=0)
            one = (raw + branch).astype(jnp.bfloat16)
            one_ref[r] = one
            normed = layer_normed(one.astype(jnp.float32))
            wide_ref[:, at * ROWS : (at + 1) * ROWS] = normed.reshape(chips, ROWS, channels)
            masked = place[FIRST_ROW + far] + r >= place[VALID]
            bias_rows(wb_ref, 1, normed.astype(jnp.bfloat16), at, 2 * count, masked, rows_ref)
    rows = 2 * count * ROWS
    sent_ref[:, :rows] = wide_ref[...].astype(jnp.bfloat16)
    for x in range(X // 2):
        quarter = rows_ref[:, x * QUARTER : (x + 1) * QUARTER].astype(jnp.bfloat16)
        sent_ref[x * YZ : (x + 1) * YZ, rows:] = jnp.broadcast_to(
            quarter[None], (YZ,) + quarter.shape
        )


def finish_columns(own_ref, got_ref, w_ref, out_ref):
    chips, rows, width, channels = own_ref.shape
    gated = own_ref[...].astype(jnp.float32) + got_ref[...].astype(jnp.float32)
    gated = gated.reshape(chips * rows * width, channels).astype(jnp.bfloat16)
    branch = jnp.dot(gated, w_ref[1], preferred_element_type=jnp.float32)
    out_ref[...] = branch.reshape(chips, rows, width, channels).astype(jnp.bfloat16)


def add_back(place, near_ref, got_ref, back_ref, out_ref):
    chips, count, width, channels = back_ref.shape
    lower = place[UPPER] == 0
    for r in range(count):
        back = back_ref[:, r].astype(jnp.float32).reshape(chips * width, channels)
        near, got = near_ref[r].astype(jnp.float32), got_ref[r].astype(jnp.float32)
        one = jnp.concatenate([jnp.where(lower, near, got), jnp.where(lower, got, near)], axis=0)
        out_ref[r] = outer_order(one + back).astype(jnp.bfloat16)


def swap(array):
    return lax.ppermute(array, "c", [(0, 1), (1, 0)])


def spread_bias(core, mine, other):
    got = swap(other)
    rows, tokens = mine.shape
    mine, got = (a.reshape(2, rows // 2, tokens) for a in (mine, got))
    low, high = jnp.where(core == 0, mine, got), jnp.where(core == 0, got, mine)
    bias = jnp.stack([low, high], axis=1).reshape(2 * rows, tokens)
    return lax.all_to_all(jnp.broadcast_to(bias[None], (YZ,) + bias.shape), ("y", "z"), 0, 0)


def whole(shape):
    return pl.BlockSpec(shape, lambda s: (0,) * len(shape))


def struct(shape, kind=jnp.bfloat16):
    return jax.ShapeDtypeStruct(shape, kind)


def shards(pair, valid, w_query, w_key, w_value, w_gate, w_bias, w_out):
    count, tokens, channels = pair.shape
    core, upper, lower = (lax.axis_index(name) for name in ("c", "xh", "xl"))
    x = 2 * upper + lower
    chip = lax.axis_index("y") * lax.axis_size("z") + lax.axis_index("z")
    first_rows = [(chip * X + (x ^ s)) * ROWS + core * count for s in (0, 2)]
    spots = [x ^ s for s in range(X)]
    place = jnp.stack([core, upper, valid[0]] + spots + first_rows + [lower, 1 - lower])
    place = place.astype(jnp.int32)
    wb = jnp.swapaxes(w_bias, 1, 2)
    weights = [w_query, w_key, w_value, w_gate]
    piece = (X * YZ, count, ROWS, channels)
    rows = (ROWS, tokens, channels)
    held = (count, tokens, channels)
    half = struct((ROWS, tokens))
    bias_scratch = pltpu.VMEM((4 * count, tokens), jnp.float32)
    projections = [
        struct(rows),
        struct((ROWS, channels, tokens)),
        struct(rows),
        struct(rows, jnp.float32),
    ]

    far = along_x(pair, 2)
    normed, mine, other = pl.pallas_call(
        prepare_rows,
        in_specs=[SMEM, VMEM, VMEM],
        out_specs=[VMEM] * 3,
        out_shape=[struct(held), half, half],
        scratch_shapes=[bias_scratch],
        compiler_params=params(),
        cost_estimate=cost(1 << 25, 2 << 20),
    )(place, pair, wb)
    gathered = spread_bias(core, mine, other)
    packed = struct((channels, 4 * channels))
    first_weights, next_weights = pl.pallas_call(
        pack_weights,
        in_specs=[VMEM] * 4,
        out_specs=[VMEM] * 2,
        out_shape=[packed, packed],
        compiler_params=params(),
    )(*weights)
    def project_group(array):
        *projected, done = pl.pallas_call(
            project_rows,
            in_specs=[SMEM, VMEM, VMEM, VMEM],
            out_specs=[VMEM] * 5,
            out_shape=projections + [struct((8, 128), jnp.float32)],
            compiler_params=params(),
            cost_estimate=cost(8 * ROWS * tokens * channels * channels, 6 << 20),
        )(place, swap(array), array, first_weights)
        return projected, done

    projected, done = project_group(normed)
    far, done = lax.optimization_barrier((far, done))
    normed_far = pl.pallas_call(
        prepare_far,
        in_specs=[VMEM],
        out_specs=VMEM,
        out_shape=struct(held),
        compiler_params=params(),
        cost_estimate=cost(1 << 24, 1 << 20),
    )(far)
    projected_far, done = project_group(normed_far)
    gathered, done = lax.optimization_barrier((gathered, done))
    projected = projected + projected_far
    for_sib, own = attend_all(False, place, projected, gathered)
    peers = X // 2 * YZ
    message = (peers, 2 * count * ROWS + 8 * count, channels)
    half_rows = struct((count, HALF, channels))
    near, other, sent = pl.pallas_call(
        finish_rows,
        in_specs=[SMEM] + [VMEM] * 6,
        out_specs=[VMEM] * 3,
        out_shape=[half_rows, half_rows, struct(message)],
        scratch_shapes=[
            pltpu.VMEM((8 * count, HALF), jnp.float32),
            pltpu.VMEM((peers, 2 * count * ROWS, channels), jnp.float32),
        ],
        compiler_params=params(),
        cost_estimate=cost(1 << 27, 3 << 20),
    )(place, own, swap(for_sib), pair, far, w_out, wb)

    got = lax.all_to_all(sent, ("xl", "y", "z"), 0, 0)
    got_near = along_x(other, 2)
    got, got_near = lax.optimization_barrier((got, got_near))
    got_sib = swap(got)
    quarter = pl.pallas_call(
        turn_bias,
        in_specs=[SMEM, VMEM, VMEM],
        out_specs=VMEM,
        out_shape=struct((2, QUARTER, tokens)),
        scratch_shapes=[pltpu.VMEM((2, X, YZ, ROWS, QUARTER), jnp.float32)],
        compiler_params=params(),
        cost_estimate=cost(1 << 20, 3 << 20),
    )(place, got, got_sib)
    projected = pl.pallas_call(
        project_columns,
        in_specs=[SMEM] + [VMEM] * 3,
        out_specs=[VMEM] * 4,
        out_shape=projections,
        scratch_shapes=[pltpu.VMEM((X, YZ, 2, count, ROWS, channels), jnp.float32)],
        compiler_params=params(),
        cost_estimate=cost(8 * ROWS * tokens * channels * channels, 6 << 20),
    )(place, got, got_sib, next_weights)
    for_sib, own = attend_all(True, place, projected, quarter)
    branch = pl.pallas_call(
        finish_columns,
        in_specs=[VMEM] * 3,
        out_specs=VMEM,
        out_shape=struct(piece),
        compiler_params=params(),
    )(own, swap(for_sib), w_out)
    back = lax.all_to_all(branch, X_AXES + ("y", "z"), 0, 0)
    return pl.pallas_call(
        add_back,
        in_specs=[SMEM, VMEM, VMEM, VMEM],
        out_specs=VMEM,
        out_shape=struct(held),
        compiler_params=params(),
    )(place, near, got_near, back)


def solution(mesh):
    fine = Mesh(mesh.devices.reshape(2, 8, 2, 2, 2, 2), ("y", "z", "xh", "xl", "c", "dp"))
    held = P(("dp", "y", "z", "xh", "xl", "c"), None, None)
    return jax.shard_map(
        shards,
        mesh=fine,
        in_specs=(held, P("dp"), P(), P(), P(), P(), P(), P()),
        out_specs=held,
        check_vma=False,
    )
```

```python
import functools
import math

import jax
import jax.numpy as jnp
from jax import lax
from jax.experimental import pallas as pl
from jax.experimental.pallas import tpu as pltpu
from jax.sharding import Mesh, PartitionSpec as P

HEAD_DIM = 32
EPSILON = 1e-05
MASKED = -1000000000.0

X, YZ, ROWS = 4, 16, 8
QUARTER = YZ * ROWS

SMEM = pl.BlockSpec(memory_space=pltpu.SMEM)
VMEM = pl.BlockSpec(memory_space=pltpu.VMEM)

HALF = 2 * QUARTER

CORE, UPPER, VALID, SPOT, FIRST_ROW, LOCAL = 0, 1, 2, 3, 7, 9
X_AXES = ("xh", "xl")


def params(mebibytes=12):
    return pltpu.CompilerParams(vmem_limit_bytes=mebibytes * 1024 * 1024)


def cost(flops, nbytes, exps=0):
    return pl.CostEstimate(flops=flops, bytes_accessed=nbytes, transcendentals=exps)


def inner_order(rows):
    return jnp.concatenate(inner_quarters(rows), axis=0)


def inner_quarters(rows):
    parts = rows.reshape(YZ, X, ROWS, rows.shape[-1])
    return [parts[:, x].reshape(QUARTER, -1) for x in range(X)]


def outer_order(rows):
    parts = rows.reshape(X, YZ, ROWS, rows.shape[-1])
    return jnp.stack([parts[x] for x in range(X)], axis=1).reshape(rows.shape)


def layer_normed(wide):
    center = jnp.mean(wide, axis=-1, keepdims=True)
    moved = wide - center
    spread = jnp.mean(jnp.square(moved), axis=-1, keepdims=True)
    return moved * lax.rsqrt(spread + EPSILON)


def bias_rows(wb_ref, step, normed, r, count, masked, rows_ref):
    four = lax.dot_general(
        wb_ref[step], normed, (((1,), (1,)), ((), ())), preferred_element_type=jnp.float32
    )
    four = jnp.where(masked, MASKED, four)
    for h in range(four.shape[0]):
        rows_ref[h * count + r : h * count + r + 1, :] = four[h : h + 1]


def prepare_rows(place, pair_ref, wb_ref, normed_ref, mine_ref, other_ref, rows_ref):
    count, tokens, _ = pair_ref.shape
    lane = lax.broadcasted_iota(jnp.int32, (1, tokens), 1)
    x, rest = lane // QUARTER, lane % QUARTER
    token = ((rest // ROWS) * X + x) * ROWS + rest % ROWS
    masked = token >= place[VALID]
    for r in range(count):
        wide = inner_order(pair_ref[r].astype(jnp.float32))
        normed = layer_normed(wide).astype(jnp.bfloat16)
        normed_ref[r] = normed
        bias_rows(wb_ref, 0, normed, r, count, masked, rows_ref)
    low, high = rows_ref[: 2 * count], rows_ref[2 * count :]
    first = place[CORE] == 0
    mine_ref[...] = jnp.where(first, low, high).astype(jnp.bfloat16)
    other_ref[...] = jnp.where(first, high, low).astype(jnp.bfloat16)


def prepare_far(far_ref, normed_ref):
    for r in range(far_ref.shape[0]):
        wide = inner_order(far_ref[r].astype(jnp.float32))
        normed_ref[r] = layer_normed(wide).astype(jnp.bfloat16)


def project(core, normed, asking, weights):
    tokens, channels = normed.shape
    kept, asked = weights[:, : 2 * channels], weights[:, 2 * channels :]
    held = jnp.dot(normed, kept, preferred_element_type=jnp.float32)
    asked = jnp.dot(asking, asked, preferred_element_type=jnp.float32)
    query = (asked[:, :channels] * (1.0 / math.sqrt(HEAD_DIM))).astype(jnp.bfloat16)
    gate = jax.nn.sigmoid(asked[:, channels:])
    key_t = held[:, :channels].astype(jnp.bfloat16).T
    half = lax.broadcasted_iota(jnp.int32, (tokens, channels), 1) // (2 * HEAD_DIM)
    value = jnp.where(half == core, held[:, channels:], 1.0)
    return query, key_t, value.astype(jnp.bfloat16), gate


def pack_weights(wq, wk, wv, wg, first_ref, next_ref):
    for step, ref in enumerate((first_ref, next_ref)):
        ref[...] = jnp.concatenate([w[step] for w in (wk, wv, wq, wg)], axis=1)


def project_rows(place, *refs):
    groups, (w_ref, query_ref, key_ref, value_ref, gate_ref) = refs[:-5], refs[-5:]
    asking = pl.ds(pl.multiple_of(place[UPPER] * HALF, HALF), HALF)
    for g, ref in enumerate(groups):
        count = ref.shape[0]
        for r in range(count):
            out = project(place[CORE], ref[r], ref[r, asking, :], w_ref[...])
            at = g * count + r
            query_ref[at], key_ref[at], value_ref[at], gate_ref[at] = out


def received_quarters(place):
    upper = place[UPPER]
    return [
        (x, far, 2 * (1 - upper if far else upper) + x) for x in range(X // 2) for far in range(2)
    ]


def project_columns(place, own_in, sib_in, w_ref, near_ref, got_ref, query_ref, key_ref, value_ref, gate_ref, one_ref, cols_ref):
    core = place[CORE]
    _, _, _, count, width, channels = cols_ref.shape
    for ref, at in ((own_in, core), (sib_in, 1 - core)):
        part = ref[:, : 2 * count * width, :].astype(jnp.float32)
        part = part.reshape(X // 2, YZ, 2, count, width, channels)
        for x, far, quarter in received_quarters(place):
            cols_ref[pl.ds(quarter, 1), :, pl.ds(at, 1)] = part[x, :, far][None, :, None]
    flat = cols_ref.reshape(X * YZ * 2 * count, width, channels)
    for j in range(width):
        normed = flat[:, j, :].astype(jnp.bfloat16)
        out = project(core, normed, normed, w_ref[...])
        query_ref[j], key_ref[j], value_ref[j], gate_ref[j] = out
    lower = place[UPPER] == 0
    for r in range(count):
        near, got = near_ref[r].astype(jnp.float32), got_ref[r].astype(jnp.float32)
        one = jnp.concatenate([jnp.where(lower, near, got), jnp.where(lower, got, near)], axis=0)
        one_ref[r] = outer_order(one).astype(jnp.bfloat16)


def turn_bias(place, own_in, sib_in, out_ref, keyed_ref):
    first = place[CORE] == 0
    _, _, _, width, _ = keyed_ref.shape
    count = width // 2
    parts = []
    for ref in (own_in, sib_in):
        rows = ref[:, 2 * count * width :, :].astype(jnp.float32)
        middle = rows.shape[1] // 2
        parts.append(jnp.where(first, rows[:, :middle], rows[:, middle:]))
    own, sib = parts
    low, high = jnp.where(first, own, sib), jnp.where(first, sib, own)
    for h in range(2):
        for x, far, quarter in received_quarters(place):
            at = (2 * h + far) * count
            for core, part in enumerate((low, high)):
                piece = part[x * YZ : (x + 1) * YZ, at : at + count]
                keyed_ref[h, pl.ds(quarter, 1), :, core * count : (core + 1) * count] = piece[None]
        keyed = keyed_ref[h].reshape(X * YZ * width, -1)
        out_ref[h] = keyed.T.astype(jnp.bfloat16)


def attend(core, units, count, channels):
    head = lax.broadcasted_iota(jnp.int32, (count, channels), 1) // HEAD_DIM
    mine = head // 2 == core

    def scores(unit):
        query, key_t = unit[0](), unit[1]()
        zero = jnp.zeros_like(query)
        both = [jnp.where(head == 2 * core + h, query, zero) for h in range(2)]
        return jnp.dot(
            jnp.concatenate(both, axis=0), key_t, preferred_element_type=jnp.float32
        )

    def finish(unit, weight):
        _, _, _, value, gate, put = unit
        out = jnp.dot(weight, value(), preferred_element_type=jnp.float32)
        total = jnp.where(head % 2 == 0, out[:count], out[count:])
        sums = pltpu.roll(total, channels // 2, 1)
        put(jnp.where(mine, gate() * total / sums, 0.0))

    pending = None
    following = scores(units[0])
    for i, unit in enumerate(units):
        score = following
        if i + 1 < len(units):
            following = scores(units[i + 1])
        score = score + unit[2]().reshape(score.shape)
        highest = jnp.max(score, axis=-1, keepdims=True)
        weight = jnp.exp(score - highest).astype(jnp.bfloat16)
        if pending is not None:
            finish(*pending)
        pending = (unit, weight)
    finish(*pending)


def attend_quarters(steps, columns, parts, place, *refs):
    core = place[CORE]
    query_ref, key_ref, value_ref, gate_ref = refs[:4]
    pieces = refs[4 : 4 + len(steps)]
    wide_ref, columns_ref = (refs[-2], refs[-1]) if columns else (refs[-1], None)
    outs = refs[-2 - len(parts) : -2] if columns else refs[-1 - len(parts) : -1]
    half = ROWS // 2
    units = []
    for i, (s, piece_ref) in enumerate(zip(steps, pieces)):
        wide = piece_ref[...].astype(jnp.float32)
        for h in range(2):
            rows = wide[h] if columns else wide[:, h * ROWS : (h + 1) * ROWS]
            wide_ref[i, h] = rows.reshape(wide_ref.shape[2:])
        spot = place[(SPOT if columns else LOCAL) + s]
        span = pl.ds(pl.multiple_of(spot * QUARTER, QUARTER), QUARTER)

        def unit(row, put, i=i, span=span):
            return (
                lambda: query_ref[row, span, :],
                lambda: key_ref[row],
                lambda: wide_ref[i],
                lambda: value_ref[row],
                lambda: gate_ref[row, span, :],
                put,
            )

        if columns:
            for j in range(ROWS):

                def put(value, i=i, j=j):
                    columns_ref.reshape(len(steps), QUARTER, ROWS, -1)[i, :, j, :] = value

                units.append(unit(j, put))
        else:
            for part, ref in zip(parts, outs):
                for g in range(2):
                    for r in range(half):

                        def put(value, ref=ref, at=g * half + r, span=span):
                            ref[at, span, :] = value.astype(jnp.bfloat16)

                        units.append(unit(g * ROWS + part * half + r, put))
    attend(core, units, QUARTER, outs[0].shape[-1])
    if columns:
        for i, s in enumerate(steps):
            chips = pl.ds(place[SPOT + s] * YZ, YZ)
            for ref, at in zip(outs, (1 - core, core)):
                ref[chips] = columns_ref[i, :, pl.ds(at, 1)][:, 0].astype(jnp.bfloat16)


def attend_some(steps, columns, parts, place, projected, pieces, outs):
    rows, channels, tokens = projected[1].shape
    scratch = [pltpu.VMEM((len(steps), 2, QUARTER, tokens), jnp.float32)]
    if columns:
        shape = struct((X * YZ, rows // 2, rows, channels))
        scratch.append(pltpu.VMEM((len(steps), YZ, 2, rows // 2, rows, channels), jnp.float32))
    else:
        shape = struct((rows // 2, HALF, channels))
    operands = [place, *projected, *pieces]
    aliases = {}
    if outs is not None:
        aliases = {len(operands) + i: i for i in range(len(parts))}
        operands += list(outs)
    units = len(steps) * rows * len(parts)
    return pl.pallas_call(
        functools.partial(attend_quarters, steps, columns, parts),
        in_specs=[SMEM] + [VMEM] * (len(operands) - 1),
        out_specs=[VMEM] * len(parts),
        scratch_shapes=scratch,
        out_shape=[shape] * len(parts),
        input_output_aliases=aliases,
        compiler_params=params(16),
        cost_estimate=cost(
            units * 4 * QUARTER * tokens * channels, 4 << 20, units * QUARTER * tokens
        ),
    )(*operands)


def along_x(array, s):
    return lax.ppermute(array, X_AXES, [(i, i ^ s) for i in range(X)])


def attend_rows(place, projected, piece):
    moved = along_x(piece, 1)
    for_sib, own = attend_some((0,), False, (0, 1), place, projected, [piece], None)
    (for_sib,) = attend_some((1,), False, (0,), place, projected, [moved], [for_sib])
    got = swap(for_sib)
    (own,) = attend_some((1,), False, (1,), place, projected, [moved], [own])
    return got, own


def attend_columns(place, projected, piece):
    moved = {s: along_x(piece, s) for s in (1, 3, 2)}
    outs = None
    for steps in ((0,), (1, 3), (2,)):
        pieces = [moved[s] if s else piece for s in steps]
        outs = attend_some(steps, True, (0, 1), place, projected, pieces, outs)
    for_sib, own = outs
    return swap(for_sib), own


def finish_rows(place, own_ref, got_ref, pair_ref, far_ref, w_ref, wb_ref, near_ref, other_ref, sent_ref, rows_ref, wide_ref):
    count, half, channels = near_ref.shape
    chips = sent_ref.shape[0]
    lower = place[UPPER] == 0
    for far, (raw_ref, one_ref) in enumerate(((pair_ref, near_ref), (far_ref, other_ref))):
        for r in range(count):
            at = far * count + r
            gated = own_ref[at] + got_ref[at]
            branch = jnp.dot(gated, w_ref[0], preferred_element_type=jnp.float32)
            q = inner_quarters(raw_ref[r].astype(jnp.float32))
            raw = jnp.concatenate([jnp.where(lower, q[x], q[2 + x]) for x in range(2)], axis=0)
            one = (raw + branch).astype(jnp.bfloat16)
            one_ref[r] = one
            normed = layer_normed(one.astype(jnp.float32))
            wide_ref[:, at * ROWS : (at + 1) * ROWS] = normed.reshape(chips, ROWS, channels)
            masked = place[FIRST_ROW + far] + r >= place[VALID]
            bias_rows(wb_ref, 1, normed.astype(jnp.bfloat16), at, 2 * count, masked, rows_ref)
    rows = 2 * count * ROWS
    sent_ref[:, :rows] = wide_ref[...].astype(jnp.bfloat16)
    for x in range(X // 2):
        quarter = rows_ref[:, x * QUARTER : (x + 1) * QUARTER].astype(jnp.bfloat16)
        sent_ref[x * YZ : (x + 1) * YZ, rows:] = jnp.broadcast_to(
            quarter[None], (YZ,) + quarter.shape
        )


def finish_columns(own_ref, got_ref, w_ref, out_ref):
    chips, rows, width, channels = own_ref.shape
    gated = own_ref[...].astype(jnp.float32) + got_ref[...].astype(jnp.float32)
    gated = gated.reshape(chips * rows * width, channels).astype(jnp.bfloat16)
    branch = jnp.dot(gated, w_ref[1], preferred_element_type=jnp.float32)
    out_ref[...] = branch.reshape(chips, rows, width, channels).astype(jnp.bfloat16)


def add_back(one_ref, back_ref, out_ref):
    chips, count, width, channels = back_ref.shape
    for r in range(count):
        back = back_ref[:, r].astype(jnp.float32).reshape(chips * width, channels)
        total = one_ref[r].astype(jnp.float32) + outer_order(back)
        out_ref[r] = total.astype(jnp.bfloat16)


def swap(array):
    return lax.ppermute(array, "c", [(0, 1), (1, 0)])


def spread_bias(core, mine, other):
    got = swap(other)
    rows, tokens = mine.shape
    mine, got = (a.reshape(2, rows // 2, tokens) for a in (mine, got))
    low, high = jnp.where(core == 0, mine, got), jnp.where(core == 0, got, mine)
    bias = jnp.stack([low, high], axis=1).reshape(2 * rows, tokens)
    return lax.all_to_all(jnp.broadcast_to(bias[None], (YZ,) + bias.shape), ("y", "z"), 0, 0)


def whole(shape):
    return pl.BlockSpec(shape, lambda s: (0,) * len(shape))


def struct(shape, kind=jnp.bfloat16):
    return jax.ShapeDtypeStruct(shape, kind)


def shards(pair, valid, w_query, w_key, w_value, w_gate, w_bias, w_out):
    count, tokens, channels = pair.shape
    core, upper, lower = (lax.axis_index(name) for name in ("c", "xh", "xl"))
    x = 2 * upper + lower
    chip = lax.axis_index("y") * lax.axis_size("z") + lax.axis_index("z")
    first_rows = [(chip * X + (x ^ s)) * ROWS + core * count for s in (0, 2)]
    spots = [x ^ s for s in range(X)]
    place = jnp.stack([core, upper, valid[0]] + spots + first_rows + [lower, 1 - lower])
    place = place.astype(jnp.int32)
    wb = jnp.swapaxes(w_bias, 1, 2)
    weights = [w_query, w_key, w_value, w_gate]
    piece = (X * YZ, count, ROWS, channels)
    rows = (ROWS, tokens, channels)
    held = (count, tokens, channels)
    half = struct((ROWS, tokens))
    bias_scratch = pltpu.VMEM((4 * count, tokens), jnp.float32)

    def projections(number, asking):
        return [
            struct((number, asking, channels)),
            struct((number, channels, tokens)),
            struct((number, tokens, channels)),
            struct((number, asking, channels), jnp.float32),
        ]

    far = along_x(pair, 2)
    normed, mine, other = pl.pallas_call(
        prepare_rows,
        in_specs=[SMEM, VMEM, VMEM],
        out_specs=[VMEM] * 3,
        out_shape=[struct(held), half, half],
        scratch_shapes=[bias_scratch],
        compiler_params=params(),
        cost_estimate=cost(1 << 25, 2 << 20),
    )(place, pair, wb)
    gathered = spread_bias(core, mine, other)
    packed = struct((channels, 4 * channels))
    first_weights, next_weights = pl.pallas_call(
        pack_weights,
        in_specs=[VMEM] * 4,
        out_specs=[VMEM] * 2,
        out_shape=[packed, packed],
        compiler_params=params(),
    )(*weights)
    normed_far = pl.pallas_call(
        prepare_far,
        in_specs=[VMEM],
        out_specs=VMEM,
        out_shape=struct(held),
        compiler_params=params(),
        cost_estimate=cost(1 << 24, 1 << 20),
    )(far)
    projected = pl.pallas_call(
        project_rows,
        in_specs=[SMEM] + [VMEM] * 5,
        out_specs=[VMEM] * 4,
        out_shape=projections(2 * ROWS, HALF),
        compiler_params=params(),
        cost_estimate=cost(12 * ROWS * tokens * channels * channels, 12 << 20),
    )(place, swap(normed), normed, swap(normed_far), normed_far, first_weights)
    got, own = attend_rows(place, projected, gathered)
    peers = X // 2 * YZ
    message = (peers, 2 * count * ROWS + 8 * count, channels)
    half_rows = struct((count, HALF, channels))
    near, other, sent = pl.pallas_call(
        finish_rows,
        in_specs=[SMEM] + [VMEM] * 6,
        out_specs=[VMEM] * 3,
        out_shape=[half_rows, half_rows, struct(message)],
        scratch_shapes=[
            pltpu.VMEM((8 * count, HALF), jnp.float32),
            pltpu.VMEM((peers, 2 * count * ROWS, channels), jnp.float32),
        ],
        compiler_params=params(),
        cost_estimate=cost(1 << 27, 3 << 20),
    )(place, own, got, pair, far, w_out, wb)

    got = lax.all_to_all(sent, ("xl", "y", "z"), 0, 0)
    got_near = along_x(other, 2)
    got, got_near = lax.optimization_barrier((got, got_near))
    got_sib = swap(got)
    quarter = pl.pallas_call(
        turn_bias,
        in_specs=[SMEM, VMEM, VMEM],
        out_specs=VMEM,
        out_shape=struct((2, QUARTER, tokens)),
        scratch_shapes=[pltpu.VMEM((2, X, YZ, ROWS, QUARTER), jnp.float32)],
        compiler_params=params(),
        cost_estimate=cost(1 << 20, 3 << 20),
    )(place, got, got_sib)
    *projected, one = pl.pallas_call(
        project_columns,
        in_specs=[SMEM] + [VMEM] * 5,
        out_specs=[VMEM] * 5,
        out_shape=projections(ROWS, tokens) + [struct(held)],
        scratch_shapes=[pltpu.VMEM((X, YZ, 2, count, ROWS, channels), jnp.float32)],
        compiler_params=params(),
        cost_estimate=cost(8 * ROWS * tokens * channels * channels, 6 << 20),
    )(place, got, got_sib, next_weights, near, got_near)
    got, own = attend_columns(place, projected, quarter)
    branch = pl.pallas_call(
        finish_columns,
        in_specs=[VMEM] * 3,
        out_specs=VMEM,
        out_shape=struct(piece),
        compiler_params=params(),
    )(own, got, w_out)
    back = lax.all_to_all(branch, X_AXES + ("y", "z"), 0, 0)
    return pl.pallas_call(
        add_back,
        in_specs=[VMEM, VMEM],
        out_specs=VMEM,
        out_shape=struct(held),
        compiler_params=params(),
    )(one, back)


def solution(mesh):
    fine = Mesh(mesh.devices.reshape(2, 8, 2, 2, 2, 2), ("y", "z", "xh", "xl", "c", "dp"))
    held = P(("dp", "y", "z", "xh", "xl", "c"), None, None)
    return jax.shard_map(
        shards,
        mesh=fine,
        in_specs=(held, P("dp"), P(), P(), P(), P(), P(), P()),
        out_specs=held,
        check_vma=False,
    )
```

```python
import functools
import math

import jax
import jax.numpy as jnp
from jax import lax
from jax.experimental import pallas as pl
from jax.experimental.pallas import tpu as pltpu
from jax.sharding import Mesh, PartitionSpec as P

HEAD_DIM = 32
EPSILON = 1e-05
MASKED = -1000000000.0

X, YZ, ROWS = 4, 16, 8
QUARTER = YZ * ROWS

SMEM = pl.BlockSpec(memory_space=pltpu.SMEM)
VMEM = pl.BlockSpec(memory_space=pltpu.VMEM)

HALF = 2 * QUARTER

CORE, UPPER, VALID, SPOT, FIRST_ROW, LOCAL = 0, 1, 2, 3, 7, 9
X_AXES = ("xh", "xl")


def params(mebibytes=12):
    return pltpu.CompilerParams(vmem_limit_bytes=mebibytes * 1024 * 1024)


def cost(flops, nbytes, exps=0):
    return pl.CostEstimate(flops=flops, bytes_accessed=nbytes, transcendentals=exps)


def inner_order(rows):
    return jnp.concatenate(inner_quarters(rows), axis=0)


def inner_quarters(rows):
    parts = rows.reshape(YZ, X, ROWS, rows.shape[-1])
    return [parts[:, x].reshape(QUARTER, -1) for x in range(X)]


def outer_order(rows):
    parts = rows.reshape(X, YZ, ROWS, rows.shape[-1])
    return jnp.stack([parts[x] for x in range(X)], axis=1).reshape(rows.shape)


def layer_normed(wide):
    center = jnp.mean(wide, axis=-1, keepdims=True)
    moved = wide - center
    spread = jnp.mean(jnp.square(moved), axis=-1, keepdims=True)
    return moved * lax.rsqrt(spread + EPSILON)


def head_bias(wb_ref, step, normed, masked):
    four = lax.dot_general(
        wb_ref[step], normed, (((1,), (1,)), ((), ())), preferred_element_type=jnp.float32
    )
    return jnp.where(masked, MASKED, four)


def prepare_rows(place, sib_ref, own_ref, wb_ref, normed_ref, bias_ref, rows_ref):
    count, tokens, _ = own_ref.shape
    core = place[CORE]
    lane = lax.broadcasted_iota(jnp.int32, (1, tokens), 1)
    x, rest = lane // QUARTER, lane % QUARTER
    token = ((rest // ROWS) * X + x) * ROWS + rest % ROWS
    masked = token >= place[VALID]
    for half, (ref, at) in enumerate(((sib_ref, 1 - core), (own_ref, core))):
        for r in range(count):
            wide = inner_order(ref[r].astype(jnp.float32))
            normed = layer_normed(wide).astype(jnp.bfloat16)
            normed_ref[half * count + r] = normed
            four = head_bias(wb_ref, 0, normed, masked)
            for h in range(2):
                row = jnp.where(core == 0, four[h : h + 1], four[2 + h : 3 + h])
                rows_ref[pl.ds(h * ROWS + at * count + r, 1), :] = row
    bias_ref[...] = rows_ref[...].astype(jnp.bfloat16)


def prepare_far(far_ref, normed_ref):
    for r in range(far_ref.shape[0]):
        wide = inner_order(far_ref[r].astype(jnp.float32))
        normed_ref[r] = layer_normed(wide).astype(jnp.bfloat16)


def project(core, normed, asking, weights):
    tokens, channels = normed.shape
    kept, asked = weights[:, : 2 * channels], weights[:, 2 * channels :]
    held = jnp.dot(normed, kept, preferred_element_type=jnp.float32)
    asked = jnp.dot(asking, asked, preferred_element_type=jnp.float32)
    query = (asked[:, :channels] * (1.0 / math.sqrt(HEAD_DIM))).astype(jnp.bfloat16)
    gate = jax.nn.sigmoid(asked[:, channels:])
    key_t = held[:, :channels].astype(jnp.bfloat16).T
    half = lax.broadcasted_iota(jnp.int32, (tokens, channels), 1) // (2 * HEAD_DIM)
    value = jnp.where(half == core, held[:, channels:], 1.0)
    return query, key_t, value.astype(jnp.bfloat16), gate


def pack_weights(wq, wk, wv, wg, first_ref, next_ref):
    for step, ref in enumerate((first_ref, next_ref)):
        ref[...] = jnp.concatenate([w[step] for w in (wk, wv, wq, wg)], axis=1)


def project_rows(place, *refs):
    groups, (w_ref, query_ref, key_ref, value_ref, gate_ref) = refs[:-5], refs[-5:]
    asking = pl.ds(pl.multiple_of(place[UPPER] * HALF, HALF), HALF)
    for at, (ref, r) in enumerate((ref, r) for ref in groups for r in range(ref.shape[0])):
        out = project(place[CORE], ref[r], ref[r, asking, :], w_ref[...])
        query_ref[at], key_ref[at], value_ref[at], gate_ref[at] = out


def received_quarters(place):
    upper = place[UPPER]
    return [
        (x, far, 2 * (1 - upper if far else upper) + x) for x in range(X // 2) for far in range(2)
    ]


def project_columns(place, own_in, sib_in, w_ref, near_ref, got_ref, query_ref, key_ref, value_ref, gate_ref, one_ref, cols_ref):
    core = place[CORE]
    _, _, _, count, width, channels = cols_ref.shape
    for ref, at in ((own_in, core), (sib_in, 1 - core)):
        part = ref[:, : 2 * count * width, :].astype(jnp.float32)
        part = part.reshape(X // 2, YZ, 2, count, width, channels)
        for x, far, quarter in received_quarters(place):
            cols_ref[pl.ds(quarter, 1), :, pl.ds(at, 1)] = part[x, :, far][None, :, None]
    flat = cols_ref.reshape(X * YZ * 2 * count, width, channels)
    for j in range(width):
        normed = flat[:, j, :].astype(jnp.bfloat16)
        out = project(core, normed, normed, w_ref[...])
        query_ref[j], key_ref[j], value_ref[j], gate_ref[j] = out
    lower = place[UPPER] == 0
    for r in range(count):
        near, got = near_ref[r].astype(jnp.float32), got_ref[r].astype(jnp.float32)
        one = jnp.concatenate([jnp.where(lower, near, got), jnp.where(lower, got, near)], axis=0)
        one_ref[r] = outer_order(one).astype(jnp.bfloat16)


def turn_bias(place, own_in, sib_in, out_ref, keyed_ref):
    first = place[CORE] == 0
    _, _, _, width, _ = keyed_ref.shape
    count = width // 2
    parts = []
    for ref in (own_in, sib_in):
        rows = ref[:, 2 * count * width :, :].astype(jnp.float32)
        middle = rows.shape[1] // 2
        parts.append(jnp.where(first, rows[:, :middle], rows[:, middle:]))
    own, sib = parts
    low, high = jnp.where(first, own, sib), jnp.where(first, sib, own)
    for h in range(2):
        for x, far, quarter in received_quarters(place):
            at = (2 * h + far) * count
            for core, part in enumerate((low, high)):
                piece = part[x * YZ : (x + 1) * YZ, at : at + count]
                keyed_ref[h, pl.ds(quarter, 1), :, core * count : (core + 1) * count] = piece[None]
        keyed = keyed_ref[h].reshape(X * YZ * width, -1)
        out_ref[h] = keyed.T.astype(jnp.bfloat16)


def attend(core, units, count, channels):
    head = lax.broadcasted_iota(jnp.int32, (count, channels), 1) // HEAD_DIM
    mine = head // 2 == core

    def scores(unit):
        query, key_t = unit[0](), unit[1]()
        zero = jnp.zeros_like(query)
        both = [jnp.where(head == 2 * core + h, query, zero) for h in range(2)]
        return jnp.dot(
            jnp.concatenate(both, axis=0), key_t, preferred_element_type=jnp.float32
        )

    def finish(unit, weight):
        _, _, _, value, gate, put = unit
        out = jnp.dot(weight, value(), preferred_element_type=jnp.float32)
        total = jnp.where(head % 2 == 0, out[:count], out[count:])
        sums = pltpu.roll(total, channels // 2, 1)
        put(jnp.where(mine, gate() * total / sums, 0.0))

    pending = None
    following = scores(units[0])
    for i, unit in enumerate(units):
        score = following
        if i + 1 < len(units):
            following = scores(units[i + 1])
        score = score + unit[2]().reshape(score.shape)
        highest = jnp.max(score, axis=-1, keepdims=True)
        weight = jnp.exp(score - highest).astype(jnp.bfloat16)
        if pending is not None:
            finish(*pending)
        pending = (unit, weight)
    finish(*pending)


def attend_quarters(steps, columns, parts, place, *refs):
    core = place[CORE]
    query_ref, key_ref, value_ref, gate_ref = refs[:4]
    pieces = refs[4 : 4 + len(steps)]
    wide_ref, columns_ref = (refs[-2], refs[-1]) if columns else (refs[-1], None)
    outs = refs[-2 - len(parts) : -2] if columns else refs[-1 - len(parts) : -1]
    half = ROWS // 2
    units = []
    for i, (s, piece_ref) in enumerate(zip(steps, pieces)):
        wide = piece_ref[...].astype(jnp.float32)
        for h in range(2):
            rows = wide[h] if columns else wide[:, h * ROWS : (h + 1) * ROWS]
            wide_ref[i, h] = rows.reshape(wide_ref.shape[2:])
        spot = place[(SPOT if columns else LOCAL) + s]
        span = pl.ds(pl.multiple_of(spot * QUARTER, QUARTER), QUARTER)

        def unit(row, put, i=i, span=span):
            return (
                lambda: query_ref[row, span, :],
                lambda: key_ref[row],
                lambda: wide_ref[i],
                lambda: value_ref[row],
                lambda: gate_ref[row, span, :],
                put,
            )

        if columns:
            for j in range(ROWS):

                def put(value, i=i, j=j):
                    columns_ref.reshape(len(steps), QUARTER, ROWS, -1)[i, :, j, :] = value

                units.append(unit(j, put))
        else:
            for part, ref in zip(parts, outs):
                for g in range(2):
                    for r in range(half):

                        def put(value, ref=ref, at=g * half + r, span=span):
                            ref[at, span, :] = value.astype(jnp.bfloat16)

                        units.append(unit(g * ROWS + part * half + r, put))
    attend(core, units, QUARTER, outs[0].shape[-1])
    if columns:
        for i, s in enumerate(steps):
            chips = pl.ds(place[SPOT + s] * YZ, YZ)
            for ref, at in zip(outs, (1 - core, core)):
                ref[chips] = columns_ref[i, :, pl.ds(at, 1)][:, 0].astype(jnp.bfloat16)


def attend_some(steps, columns, parts, place, projected, pieces, outs):
    rows, channels, tokens = projected[1].shape
    scratch = [pltpu.VMEM((len(steps), 2, QUARTER, tokens), jnp.float32)]
    if columns:
        shape = struct((X * YZ, rows // 2, rows, channels))
        scratch.append(pltpu.VMEM((len(steps), YZ, 2, rows // 2, rows, channels), jnp.float32))
    else:
        shape = struct((rows // 2, HALF, channels))
    operands = [place, *projected, *pieces]
    aliases = {}
    if outs is not None:
        aliases = {len(operands) + i: i for i in range(len(parts))}
        operands += list(outs)
    units = len(steps) * rows * len(parts)
    return pl.pallas_call(
        functools.partial(attend_quarters, steps, columns, parts),
        in_specs=[SMEM] + [VMEM] * (len(operands) - 1),
        out_specs=[VMEM] * len(parts),
        scratch_shapes=scratch,
        out_shape=[shape] * len(parts),
        input_output_aliases=aliases,
        compiler_params=params(16),
        cost_estimate=cost(
            units * 4 * QUARTER * tokens * channels, 4 << 20, units * QUARTER * tokens
        ),
    )(*operands)


def along_x(array, s):
    return lax.ppermute(array, X_AXES, [(i, i ^ s) for i in range(X)])


def attend_rows(place, projected, piece):
    moved = along_x(piece, 1)
    for_sib, own = attend_some((0,), False, (0, 1), place, projected, [piece], None)
    (for_sib,) = attend_some((1,), False, (0,), place, projected, [moved], [for_sib])
    got = swap(for_sib)
    (own,) = attend_some((1,), False, (1,), place, projected, [moved], [own])
    return got, own


def attend_columns(place, projected, piece):
    moved = {s: along_x(piece, s) for s in (1, 3, 2)}
    outs = None
    for steps in ((0,), (3, 1), (2,)):
        pieces = [moved[s] if s else piece for s in steps]
        outs = attend_some(steps, True, (0, 1), place, projected, pieces, outs)
    for_sib, own = outs
    return swap(for_sib), own


def finish_rows(place, own_ref, got_ref, pair_ref, far_ref, w_ref, wb_ref, near_ref, other_ref, sent_ref, rows_ref, wide_ref):
    count, half, channels = near_ref.shape
    chips = sent_ref.shape[0]
    lower = place[UPPER] == 0
    for far, (raw_ref, one_ref) in enumerate(((pair_ref, near_ref), (far_ref, other_ref))):
        for r in range(count):
            at = far * count + r
            gated = own_ref[at] + got_ref[at]
            branch = jnp.dot(gated, w_ref[0], preferred_element_type=jnp.float32)
            q = inner_quarters(raw_ref[r].astype(jnp.float32))
            raw = jnp.concatenate([jnp.where(lower, q[x], q[2 + x]) for x in range(2)], axis=0)
            one = (raw + branch).astype(jnp.bfloat16)
            one_ref[r] = one
            normed = layer_normed(one.astype(jnp.float32))
            wide_ref[:, at * ROWS : (at + 1) * ROWS] = normed.reshape(chips, ROWS, channels)
            masked = place[FIRST_ROW + far] + r >= place[VALID]
            four = head_bias(wb_ref, 1, normed.astype(jnp.bfloat16), masked)
            for h in range(4):
                spot = 2 * count * h + at
                rows_ref[spot : spot + 1, :] = four[h : h + 1]
    rows = 2 * count * ROWS
    sent_ref[:, :rows] = wide_ref[...].astype(jnp.bfloat16)
    for x in range(X // 2):
        quarter = rows_ref[:, x * QUARTER : (x + 1) * QUARTER].astype(jnp.bfloat16)
        sent_ref[x * YZ : (x + 1) * YZ, rows:] = jnp.broadcast_to(
            quarter[None], (YZ,) + quarter.shape
        )


def finish_columns(own_ref, got_ref, w_ref, out_ref):
    chips, rows, width, channels = own_ref.shape
    gated = own_ref[...].astype(jnp.float32) + got_ref[...].astype(jnp.float32)
    gated = gated.reshape(chips * rows * width, channels).astype(jnp.bfloat16)
    branch = jnp.dot(gated, w_ref[1], preferred_element_type=jnp.float32)
    out_ref[...] = branch.reshape(chips, rows, width, channels).astype(jnp.bfloat16)


def add_back(one_ref, back_ref, out_ref):
    chips, count, width, channels = back_ref.shape
    for r in range(count):
        back = back_ref[:, r].astype(jnp.float32).reshape(chips * width, channels)
        total = one_ref[r].astype(jnp.float32) + outer_order(back)
        out_ref[r] = total.astype(jnp.bfloat16)


def swap(array):
    return lax.ppermute(array, "c", [(0, 1), (1, 0)])


def struct(shape, kind=jnp.bfloat16):
    return jax.ShapeDtypeStruct(shape, kind)


def shards(pair, valid, w_query, w_key, w_value, w_gate, w_bias, w_out):
    count, tokens, channels = pair.shape
    core, upper, lower = (lax.axis_index(name) for name in ("c", "xh", "xl"))
    x = 2 * upper + lower
    chip = lax.axis_index("y") * lax.axis_size("z") + lax.axis_index("z")
    first_rows = [(chip * X + (x ^ s)) * ROWS + core * count for s in (0, 2)]
    spots = [x ^ s for s in range(X)]
    place = jnp.stack([core, upper, valid[0]] + spots + first_rows + [lower, 1 - lower])
    place = place.astype(jnp.int32)
    wb = jnp.swapaxes(w_bias, 1, 2)
    weights = [w_query, w_key, w_value, w_gate]
    piece = (X * YZ, count, ROWS, channels)
    rows = (ROWS, tokens, channels)
    held = (count, tokens, channels)
    bias_scratch = pltpu.VMEM((4 * count, tokens), jnp.float32)

    def projections(number, asking):
        return [
            struct((number, asking, channels)),
            struct((number, channels, tokens)),
            struct((number, tokens, channels)),
            struct((number, asking, channels), jnp.float32),
        ]

    sib = swap(pair)
    far = along_x(pair, 2)
    normed, bias = pl.pallas_call(
        prepare_rows,
        in_specs=[SMEM, VMEM, VMEM, VMEM],
        out_specs=[VMEM] * 2,
        out_shape=[struct(rows), struct((2 * ROWS, tokens))],
        scratch_shapes=[bias_scratch],
        compiler_params=params(),
        cost_estimate=cost(1 << 25, 2 << 20),
    )(place, sib, pair, wb)
    copies = jnp.broadcast_to(bias[None], (YZ,) + bias.shape)
    gathered = lax.all_to_all(copies, ("y", "z"), 0, 0)
    packed = struct((channels, 4 * channels))
    first_weights, next_weights = pl.pallas_call(
        pack_weights,
        in_specs=[VMEM] * 4,
        out_specs=[VMEM] * 2,
        out_shape=[packed, packed],
        compiler_params=params(),
    )(*weights)
    normed_far = pl.pallas_call(
        prepare_far,
        in_specs=[VMEM],
        out_specs=VMEM,
        out_shape=struct(held),
        compiler_params=params(),
        cost_estimate=cost(1 << 24, 1 << 20),
    )(far)
    projected = pl.pallas_call(
        project_rows,
        in_specs=[SMEM] + [VMEM] * 4,
        out_specs=[VMEM] * 4,
        out_shape=projections(2 * ROWS, HALF),
        compiler_params=params(),
        cost_estimate=cost(12 * ROWS * tokens * channels * channels, 12 << 20),
    )(place, normed, swap(normed_far), normed_far, first_weights)
    got, own = attend_rows(place, projected, gathered)
    peers = X // 2 * YZ
    message = (peers, 2 * count * ROWS + 8 * count, channels)
    half_rows = struct((count, HALF, channels))
    near, other, sent = pl.pallas_call(
        finish_rows,
        in_specs=[SMEM] + [VMEM] * 6,
        out_specs=[VMEM] * 3,
        out_shape=[half_rows, half_rows, struct(message)],
        scratch_shapes=[
            pltpu.VMEM((8 * count, HALF), jnp.float32),
            pltpu.VMEM((peers, 2 * count * ROWS, channels), jnp.float32),
        ],
        compiler_params=params(),
        cost_estimate=cost(1 << 27, 3 << 20),
    )(place, own, got, pair, far, w_out, wb)

    got = lax.all_to_all(sent, ("xl", "y", "z"), 0, 0)
    got_near = along_x(other, 2)
    got, got_near = lax.optimization_barrier((got, got_near))
    got_sib = swap(got)
    quarter = pl.pallas_call(
        turn_bias,
        in_specs=[SMEM, VMEM, VMEM],
        out_specs=VMEM,
        out_shape=struct((2, QUARTER, tokens)),
        scratch_shapes=[pltpu.VMEM((2, X, YZ, ROWS, QUARTER), jnp.float32)],
        compiler_params=params(),
        cost_estimate=cost(1 << 20, 3 << 20),
    )(place, got, got_sib)
    *projected, one = pl.pallas_call(
        project_columns,
        in_specs=[SMEM] + [VMEM] * 5,
        out_specs=[VMEM] * 5,
        out_shape=projections(ROWS, tokens) + [struct(held)],
        scratch_shapes=[pltpu.VMEM((X, YZ, 2, count, ROWS, channels), jnp.float32)],
        compiler_params=params(),
        cost_estimate=cost(8 * ROWS * tokens * channels * channels, 6 << 20),
    )(place, got, got_sib, next_weights, near, got_near)
    got, own = attend_columns(place, projected, quarter)
    branch = pl.pallas_call(
        finish_columns,
        in_specs=[VMEM] * 3,
        out_specs=VMEM,
        out_shape=struct(piece),
        compiler_params=params(),
    )(own, got, w_out)
    back = lax.all_to_all(branch, X_AXES + ("y", "z"), 0, 0)
    return pl.pallas_call(
        add_back,
        in_specs=[VMEM, VMEM],
        out_specs=VMEM,
        out_shape=struct(held),
        compiler_params=params(),
    )(one, back)


def solution(mesh):
    fine = Mesh(mesh.devices.reshape(2, 8, 2, 2, 2, 2), ("y", "z", "xh", "xl", "c", "dp"))
    held = P(("dp", "y", "z", "xh", "xl", "c"), None, None)
    return jax.shard_map(
        shards,
        mesh=fine,
        in_specs=(held, P("dp"), P(), P(), P(), P(), P(), P()),
        out_specs=held,
        check_vma=False,
    )
```

```python
import functools
import math

import jax
import jax.numpy as jnp
from jax import lax
from jax.experimental import pallas as pl
from jax.experimental.pallas import tpu as pltpu
from jax.sharding import Mesh, PartitionSpec as P

HEAD_DIM = 32
EPSILON = 1e-05
MASKED = -1000000000.0

X, YZ, ROWS = 4, 16, 8
QUARTER = YZ * ROWS

SMEM = pl.BlockSpec(memory_space=pltpu.SMEM)
VMEM = pl.BlockSpec(memory_space=pltpu.VMEM)

HALF = 2 * QUARTER

CORE, UPPER, VALID, SPOT, FIRST_ROW, LOCAL = 0, 1, 2, 3, 7, 9
X_AXES = ("xh", "xl")


def params(mebibytes=6):
    return pltpu.CompilerParams(vmem_limit_bytes=mebibytes * 1024 * 1024)


def cost(flops, nbytes, exps=0):
    return pl.CostEstimate(flops=flops, bytes_accessed=nbytes, transcendentals=exps)


def inner_order(rows):
    return jnp.concatenate(inner_quarters(rows), axis=0)


def inner_quarters(rows):
    parts = rows.reshape(YZ, X, ROWS, rows.shape[-1])
    return [parts[:, x].reshape(QUARTER, -1) for x in range(X)]


def outer_order(rows):
    parts = rows.reshape(X, YZ, ROWS, rows.shape[-1])
    return jnp.stack([parts[x] for x in range(X)], axis=1).reshape(rows.shape)


def layer_normed(wide):
    center = jnp.mean(wide, axis=-1, keepdims=True)
    moved = wide - center
    spread = jnp.mean(jnp.square(moved), axis=-1, keepdims=True)
    return moved * lax.rsqrt(spread + EPSILON)


def head_bias(wb_ref, step, normed, masked):
    four = lax.dot_general(
        wb_ref[step], normed, (((1,), (1,)), ((), ())), preferred_element_type=jnp.float32
    )
    return jnp.where(masked, MASKED, four)


def prepare_rows(place, sib_ref, own_ref, wb_ref, normed_ref, bias_ref, rows_ref):
    count, tokens, _ = own_ref.shape
    core = place[CORE]
    lane = lax.broadcasted_iota(jnp.int32, (1, tokens), 1)
    x, rest = lane // QUARTER, lane % QUARTER
    token = ((rest // ROWS) * X + x) * ROWS + rest % ROWS
    masked = token >= place[VALID]
    for half, (ref, at) in enumerate(((sib_ref, 1 - core), (own_ref, core))):
        for r in range(count):
            wide = inner_order(ref[r].astype(jnp.float32))
            normed = layer_normed(wide).astype(jnp.bfloat16)
            normed_ref[half * count + r] = normed
            four = head_bias(wb_ref, 0, normed, masked)
            for h in range(2):
                row = jnp.where(core == 0, four[h : h + 1], four[2 + h : 3 + h])
                rows_ref[pl.ds(h * ROWS + at * count + r, 1), :] = row
    bias_ref[...] = rows_ref[...].astype(jnp.bfloat16)


def prepare_far(far_ref, normed_ref):
    for r in range(far_ref.shape[0]):
        wide = inner_order(far_ref[r].astype(jnp.float32))
        normed_ref[r] = layer_normed(wide).astype(jnp.bfloat16)


def project(core, normed, asking, weights):
    tokens, channels = normed.shape
    kept, asked = weights[:, : 2 * channels], weights[:, 2 * channels :]
    held = jnp.dot(normed, kept, preferred_element_type=jnp.float32)
    asked = jnp.dot(asking, asked, preferred_element_type=jnp.float32)
    query = (asked[:, :channels] * (1.0 / math.sqrt(HEAD_DIM))).astype(jnp.bfloat16)
    gate = jax.nn.sigmoid(asked[:, channels:])
    key_t = held[:, :channels].astype(jnp.bfloat16).T
    half = lax.broadcasted_iota(jnp.int32, (tokens, channels), 1) // (2 * HEAD_DIM)
    value = jnp.where(half == core, held[:, channels:], 1.0)
    return query, key_t, value.astype(jnp.bfloat16), gate


def pack_weights(wq, wk, wv, wg, first_ref, next_ref):
    for step, ref in enumerate((first_ref, next_ref)):
        ref[...] = jnp.concatenate([w[step] for w in (wk, wv, wq, wg)], axis=1)


def project_rows(place, *refs):
    groups, (w_ref, query_ref, key_ref, value_ref, gate_ref) = refs[:-5], refs[-5:]
    asking = pl.ds(pl.multiple_of(place[UPPER] * HALF, HALF), HALF)
    for at, (ref, r) in enumerate((ref, r) for ref in groups for r in range(ref.shape[0])):
        out = project(place[CORE], ref[r], ref[r, asking, :], w_ref[...])
        query_ref[at], key_ref[at], value_ref[at], gate_ref[at] = out


def received_quarters(place):
    upper = place[UPPER]
    return [
        (x, far, 2 * (1 - upper if far else upper) + x) for x in range(X // 2) for far in range(2)
    ]


def project_columns(place, own_in, sib_in, w_ref, near_ref, got_ref, query_ref, key_ref, value_ref, gate_ref, one_ref, cols_ref):
    core = place[CORE]
    _, _, _, count, width, channels = cols_ref.shape
    for ref, at in ((own_in, core), (sib_in, 1 - core)):
        part = ref[:, : 2 * count * width, :].astype(jnp.float32)
        part = part.reshape(X // 2, YZ, 2, count, width, channels)
        for x, far, quarter in received_quarters(place):
            cols_ref[pl.ds(quarter, 1), :, pl.ds(at, 1)] = part[x, :, far][None, :, None]
    flat = cols_ref.reshape(X * YZ * 2 * count, width, channels)
    for j in range(width):
        normed = flat[:, j, :].astype(jnp.bfloat16)
        out = project(core, normed, normed, w_ref[...])
        query_ref[j], key_ref[j], value_ref[j], gate_ref[j] = out
    lower = place[UPPER] == 0
    for r in range(count):
        near, got = near_ref[r].astype(jnp.float32), got_ref[r].astype(jnp.float32)
        one = jnp.concatenate([jnp.where(lower, near, got), jnp.where(lower, got, near)], axis=0)
        one_ref[r] = outer_order(one).astype(jnp.bfloat16)


def turn_bias(place, own_in, sib_in, out_ref, keyed_ref):
    first = place[CORE] == 0
    _, _, _, width, _ = keyed_ref.shape
    count = width // 2
    parts = []
    for ref in (own_in, sib_in):
        rows = ref[:, 2 * count * width :, :].astype(jnp.float32)
        middle = rows.shape[1] // 2
        parts.append(jnp.where(first, rows[:, :middle], rows[:, middle:]))
    own, sib = parts
    low, high = jnp.where(first, own, sib), jnp.where(first, sib, own)
    for h in range(2):
        for x, far, quarter in received_quarters(place):
            at = (2 * h + far) * count
            for core, part in enumerate((low, high)):
                piece = part[x * YZ : (x + 1) * YZ, at : at + count]
                keyed_ref[h, pl.ds(quarter, 1), :, core * count : (core + 1) * count] = piece[None]
        keyed = keyed_ref[h].reshape(X * YZ * width, -1)
        out_ref[h] = keyed.T.astype(jnp.bfloat16)


def attend(core, units, count, channels):
    head = lax.broadcasted_iota(jnp.int32, (count, channels), 1) // HEAD_DIM
    mine = head // 2 == core

    def scores(unit):
        query, key_t = unit[0](), unit[1]()
        zero = jnp.zeros_like(query)
        both = [jnp.where(head == 2 * core + h, query, zero) for h in range(2)]
        return jnp.dot(
            jnp.concatenate(both, axis=0), key_t, preferred_element_type=jnp.float32
        )

    def finish(unit, weight):
        _, _, _, value, gate, put = unit
        out = jnp.dot(weight, value(), preferred_element_type=jnp.float32)
        total = jnp.where(head % 2 == 0, out[:count], out[count:])
        sums = pltpu.roll(total, channels // 2, 1)
        put(jnp.where(mine, gate() * total / sums, 0.0))

    pending = None
    following = scores(units[0])
    for i, unit in enumerate(units):
        score = following
        if i + 1 < len(units):
            following = scores(units[i + 1])
        score = score + unit[2]().reshape(score.shape)
        highest = jnp.max(score, axis=-1, keepdims=True)
        weight = jnp.exp(score - highest).astype(jnp.bfloat16)
        if pending is not None:
            finish(*pending)
        pending = (unit, weight)
    finish(*pending)


def attend_quarters(steps, columns, parts, place, *refs):
    core = place[CORE]
    query_ref, key_ref, value_ref, gate_ref = refs[:4]
    pieces = refs[4 : 4 + len(steps)]
    wide_ref, columns_ref = (refs[-2], refs[-1]) if columns else (refs[-1], None)
    outs = refs[-2 - len(parts) : -2] if columns else refs[-1 - len(parts) : -1]
    half = ROWS // 2
    units = []
    for i, (s, piece_ref) in enumerate(zip(steps, pieces)):
        wide = piece_ref[...].astype(jnp.float32)
        for h in range(2):
            rows = wide[h] if columns else wide[:, h * ROWS : (h + 1) * ROWS]
            wide_ref[i, h] = rows.reshape(wide_ref.shape[2:])
        spot = place[(SPOT if columns else LOCAL) + s]
        span = pl.ds(pl.multiple_of(spot * QUARTER, QUARTER), QUARTER)

        def unit(row, put, i=i, span=span):
            return (
                lambda: query_ref[row, span, :],
                lambda: key_ref[row],
                lambda: wide_ref[i],
                lambda: value_ref[row],
                lambda: gate_ref[row, span, :],
                put,
            )

        if columns:
            for j in range(ROWS):

                def put(value, i=i, j=j):
                    columns_ref.reshape(len(steps), QUARTER, ROWS, -1)[i, :, j, :] = value

                units.append(unit(j, put))
        else:
            for part, ref in zip(parts, outs):
                for g in range(2):
                    for r in range(half):

                        def put(value, ref=ref, at=g * half + r, span=span):
                            ref[at, span, :] = value.astype(jnp.bfloat16)

                        units.append(unit(g * ROWS + part * half + r, put))
    attend(core, units, QUARTER, outs[0].shape[-1])
    if columns:
        for i, s in enumerate(steps):
            chips = pl.ds(place[SPOT + s] * YZ, YZ)
            for ref, at in zip(outs, (1 - core, core)):
                ref[chips] = columns_ref[i, :, pl.ds(at, 1)][:, 0].astype(jnp.bfloat16)


def attend_some(steps, columns, parts, place, projected, pieces, outs):
    rows, channels, tokens = projected[1].shape
    scratch = [pltpu.VMEM((len(steps), 2, QUARTER, tokens), jnp.float32)]
    if columns:
        shape = struct((X * YZ, rows // 2, rows, channels))
        scratch.append(pltpu.VMEM((len(steps), YZ, 2, rows // 2, rows, channels), jnp.float32))
    else:
        shape = struct((rows // 2, HALF, channels))
    operands = [place, *projected, *pieces]
    aliases = {}
    if outs is not None:
        aliases = {len(operands) + i: i for i in range(len(parts))}
        operands += list(outs)
    units = len(steps) * rows * len(parts)
    return pl.pallas_call(
        functools.partial(attend_quarters, steps, columns, parts),
        in_specs=[SMEM] + [VMEM] * (len(operands) - 1),
        out_specs=[VMEM] * len(parts),
        scratch_shapes=scratch,
        out_shape=[shape] * len(parts),
        input_output_aliases=aliases,
        compiler_params=params(8),
        cost_estimate=cost(
            units * 4 * QUARTER * tokens * channels, 4 << 20, units * QUARTER * tokens
        ),
    )(*operands)


def along_x(array, s):
    return lax.ppermute(array, X_AXES, [(i, i ^ s) for i in range(X)])


def attend_rows(place, projected, piece):
    moved = along_x(piece, 1)
    for_sib, own = attend_some((0,), False, (0, 1), place, projected, [piece], None)
    (for_sib,) = attend_some((1,), False, (0,), place, projected, [moved], [for_sib])
    got = swap(for_sib)
    (own,) = attend_some((1,), False, (1,), place, projected, [moved], [own])
    return got, own


def attend_columns(place, projected, piece):
    moved = {s: along_x(piece, s) for s in (1, 3, 2)}
    outs = None
    for steps in ((0,), (3, 1), (2,)):
        pieces = [moved[s] if s else piece for s in steps]
        outs = attend_some(steps, True, (0, 1), place, projected, pieces, outs)
    for_sib, own = outs
    return swap(for_sib), own


def finish_rows(place, own_ref, got_ref, pair_ref, far_ref, w_ref, wb_ref, near_ref, other_ref, sent_ref, rows_ref, wide_ref):
    count, half, channels = near_ref.shape
    chips = sent_ref.shape[0]
    lower = place[UPPER] == 0
    for far, (raw_ref, one_ref) in enumerate(((pair_ref, near_ref), (far_ref, other_ref))):
        for r in range(count):
            at = far * count + r
            gated = own_ref[at] + got_ref[at]
            branch = jnp.dot(gated, w_ref[0], preferred_element_type=jnp.float32)
            q = inner_quarters(raw_ref[r].astype(jnp.float32))
            raw = jnp.concatenate([jnp.where(lower, q[x], q[2 + x]) for x in range(2)], axis=0)
            one = (raw + branch).astype(jnp.bfloat16)
            one_ref[r] = one
            normed = layer_normed(one.astype(jnp.float32))
            wide_ref[:, at * ROWS : (at + 1) * ROWS] = normed.reshape(chips, ROWS, channels)
            masked = place[FIRST_ROW + far] + r >= place[VALID]
            four = head_bias(wb_ref, 1, normed.astype(jnp.bfloat16), masked)
            for h in range(4):
                spot = 2 * count * h + at
                rows_ref[spot : spot + 1, :] = four[h : h + 1]
    rows = 2 * count * ROWS
    sent_ref[:, :rows] = wide_ref[...].astype(jnp.bfloat16)
    for x in range(X // 2):
        quarter = rows_ref[:, x * QUARTER : (x + 1) * QUARTER].astype(jnp.bfloat16)
        sent_ref[x * YZ : (x + 1) * YZ, rows:] = jnp.broadcast_to(
            quarter[None], (YZ,) + quarter.shape
        )


def finish_columns(own_ref, got_ref, w_ref, out_ref):
    chips, rows, width, channels = own_ref.shape
    gated = own_ref[...].astype(jnp.float32) + got_ref[...].astype(jnp.float32)
    gated = gated.reshape(chips * rows * width, channels).astype(jnp.bfloat16)
    branch = jnp.dot(gated, w_ref[1], preferred_element_type=jnp.float32)
    out_ref[...] = branch.reshape(chips, rows, width, channels).astype(jnp.bfloat16)


def add_back(one_ref, back_ref, out_ref):
    chips, count, width, channels = back_ref.shape
    for r in range(count):
        back = back_ref[:, r].astype(jnp.float32).reshape(chips * width, channels)
        total = one_ref[r].astype(jnp.float32) + outer_order(back)
        out_ref[r] = total.astype(jnp.bfloat16)


def swap(array):
    return lax.ppermute(array, "c", [(0, 1), (1, 0)])


def struct(shape, kind=jnp.bfloat16):
    return jax.ShapeDtypeStruct(shape, kind)


def shards(pair, valid, w_query, w_key, w_value, w_gate, w_bias, w_out):
    count, tokens, channels = pair.shape
    core, upper, lower = (lax.axis_index(name) for name in ("c", "xh", "xl"))
    x = 2 * upper + lower
    chip = lax.axis_index("y") * lax.axis_size("z") + lax.axis_index("z")
    first_rows = [(chip * X + (x ^ s)) * ROWS + core * count for s in (0, 2)]
    spots = [x ^ s for s in range(X)]
    place = jnp.stack([core, upper, valid[0]] + spots + first_rows + [lower, 1 - lower])
    place = place.astype(jnp.int32)
    wb = jnp.swapaxes(w_bias, 1, 2)
    weights = [w_query, w_key, w_value, w_gate]
    piece = (X * YZ, count, ROWS, channels)
    rows = (ROWS, tokens, channels)
    held = (count, tokens, channels)
    bias_scratch = pltpu.VMEM((4 * count, tokens), jnp.float32)

    def projections(number, asking):
        return [
            struct((number, asking, channels)),
            struct((number, channels, tokens)),
            struct((number, tokens, channels)),
            struct((number, asking, channels), jnp.float32),
        ]

    sib = swap(pair)
    far = along_x(pair, 2)
    normed, bias = pl.pallas_call(
        prepare_rows,
        in_specs=[SMEM, VMEM, VMEM, VMEM],
        out_specs=[VMEM] * 2,
        out_shape=[struct(rows), struct((2 * ROWS, tokens))],
        scratch_shapes=[bias_scratch],
        compiler_params=params(),
        cost_estimate=cost(1 << 25, 2 << 20),
    )(place, sib, pair, wb)
    copies = jnp.broadcast_to(bias[None], (YZ,) + bias.shape)
    gathered = lax.all_to_all(copies, ("y", "z"), 0, 0)
    packed = struct((channels, 4 * channels))
    first_weights, next_weights = pl.pallas_call(
        pack_weights,
        in_specs=[VMEM] * 4,
        out_specs=[VMEM] * 2,
        out_shape=[packed, packed],
        compiler_params=params(),
    )(*weights)
    normed_far = pl.pallas_call(
        prepare_far,
        in_specs=[VMEM],
        out_specs=VMEM,
        out_shape=struct(held),
        compiler_params=params(),
        cost_estimate=cost(1 << 24, 1 << 20),
    )(far)
    projected = pl.pallas_call(
        project_rows,
        in_specs=[SMEM] + [VMEM] * 4,
        out_specs=[VMEM] * 4,
        out_shape=projections(2 * ROWS, HALF),
        compiler_params=params(),
        cost_estimate=cost(12 * ROWS * tokens * channels * channels, 12 << 20),
    )(place, normed, swap(normed_far), normed_far, first_weights)
    got, own = attend_rows(place, projected, gathered)
    peers = X // 2 * YZ
    message = (peers, 2 * count * ROWS + 8 * count, channels)
    half_rows = struct((count, HALF, channels))
    near, other, sent = pl.pallas_call(
        finish_rows,
        in_specs=[SMEM] + [VMEM] * 6,
        out_specs=[VMEM] * 3,
        out_shape=[half_rows, half_rows, struct(message)],
        scratch_shapes=[
            pltpu.VMEM((8 * count, HALF), jnp.float32),
            pltpu.VMEM((peers, 2 * count * ROWS, channels), jnp.float32),
        ],
        compiler_params=params(),
        cost_estimate=cost(1 << 27, 3 << 20),
    )(place, own, got, pair, far, w_out, wb)

    got = lax.all_to_all(sent, ("xl", "y", "z"), 0, 0)
    got_near = along_x(other, 2)
    got, got_near = lax.optimization_barrier((got, got_near))
    got_sib = swap(got)
    quarter = pl.pallas_call(
        turn_bias,
        in_specs=[SMEM, VMEM, VMEM],
        out_specs=VMEM,
        out_shape=struct((2, QUARTER, tokens)),
        scratch_shapes=[pltpu.VMEM((2, X, YZ, ROWS, QUARTER), jnp.float32)],
        compiler_params=params(),
        cost_estimate=cost(1 << 20, 3 << 20),
    )(place, got, got_sib)
    *projected, one = pl.pallas_call(
        project_columns,
        in_specs=[SMEM] + [VMEM] * 5,
        out_specs=[VMEM] * 5,
        out_shape=projections(ROWS, tokens) + [struct(held)],
        scratch_shapes=[pltpu.VMEM((X, YZ, 2, count, ROWS, channels), jnp.float32)],
        compiler_params=params(),
        cost_estimate=cost(8 * ROWS * tokens * channels * channels, 6 << 20),
    )(place, got, got_sib, next_weights, near, got_near)
    got, own = attend_columns(place, projected, quarter)
    branch = pl.pallas_call(
        finish_columns,
        in_specs=[VMEM] * 3,
        out_specs=VMEM,
        out_shape=struct(piece),
        compiler_params=params(),
    )(own, got, w_out)
    back = lax.all_to_all(branch, X_AXES + ("y", "z"), 0, 0)
    return pl.pallas_call(
        add_back,
        in_specs=[VMEM, VMEM],
        out_specs=VMEM,
        out_shape=struct(held),
        compiler_params=params(),
    )(one, back)


def solution(mesh):
    fine = Mesh(mesh.devices.reshape(2, 8, 2, 2, 2, 2), ("y", "z", "xh", "xl", "c", "dp"))
    held = P(("dp", "y", "z", "xh", "xl", "c"), None, None)
    return jax.shard_map(
        shards,
        mesh=fine,
        in_specs=(held, P("dp"), P(), P(), P(), P(), P(), P()),
        out_specs=held,
        check_vma=False,
    )
```
